128 devices in a mesh: dp: 32 (over x, y, z_lo), tensor: 4 (over z_hi, core).
Axes of the slice: x: 4, y: 4, z: 4 (z_hi: 2, z_lo: 2; z = z_hi * 2 + z_lo), core: 2. Of those that a mesh axis runs over, the one named last changes fastest.
Arguments:
- states: bfloat16 [32768, 5120], P(('dp', 'tensor')), may hold values from -6 to 6
- lengths: int32 [32, 8], P('dp'), may hold values from 1 to 512, 1024 in all within a row
- norm_gain: float32 [5120], replicated, may hold values from 0.5 to 1.5
- qk_gain: float32 [2, 128], replicated, may hold values from 0.5 to 6
- q_master: float32 [5120, 4096], P('dp', 'tensor'), may hold values from -0.078125 to 0.078125
- q_grad: bfloat16 [5120, 4096], P('dp', 'tensor'), may hold values from -6 to 6
- q_moments: float32 [2, 5120, 4096], P(None, 'dp', 'tensor'), as said below
- kv_master: float32 [2, 5120, 512], P(None, 'dp', 'tensor'), may hold values from -0.078125 to 0.078125
- kv_grad: bfloat16 [2, 5120, 512], P(None, 'dp', 'tensor'), may hold values from -6 to 6
- kv_moments: float32 [2, 2, 5120, 512], P(None, None, 'dp', 'tensor'), as said below
- o_master: float32 [5120, 4096], P('dp', 'tensor'), may hold values from -0.09375 to 0.09375
- o_grad: bfloat16 [5120, 4096], P('dp', 'tensor'), may hold values from -6 to 6
- o_moments: float32 [2, 5120, 4096], P(None, 'dp', 'tensor'), as said below
Outputs:
- scored: bfloat16 [32768, 5120], P(('dp', 'tensor'))
- q_new: float32 [5120, 4096], P('dp', 'tensor')
- q_moments_new: float32 [2, 5120, 4096], P(None, 'dp', 'tensor')
- kv_new: float32 [2, 5120, 512], P(None, 'dp', 'tensor')
- kv_moments_new: float32 [2, 2, 5120, 512], P(None, None, 'dp', 'tensor')
- o_new: float32 [5120, 4096], P('dp', 'tensor')
- o_moments_new: float32 [2, 5120, 4096], P(None, 'dp', 'tensor')
The draws below stay inside these ranges and needn't reach their ends.
Inputs may be any that keep to these rules, and one draw needn't show every extreme that they name: Each group's 8 lengths sum to 1024, and the longest of each group is exactly 512. `q_moments`: the second moments (index 1 of the first dimension) lie in 0.25 to 4. `kv_moments`: the second moments (index 1 of the first dimension) lie in 0.25 to 4. `o_moments`: the second moments (index 1 of the first dimension) lie in 0.25 to 4.
All inputs are finite; a program needn't handle non-finite values.
Results may differ from the reference program's by a relative error of at most 0.019.
The reference program's roundings to bfloat16 on the way count: a program that leaves them out, or rounds other values in their place, can miss the bound.
Values may be sent and summed in bfloat16 or wider, within the bound.
A program may use at most 128 MiB of HBM per device.

```python
import math
import jax
import jax.numpy as jnp
import numpy as np
from jax import lax

D = 5120
HEADS = 32
KV_HEADS = 4
HEAD = 128
TOK_GROUP = 1024
SEQ_GROUP = 8
GROUPS = 32
TOKENS = 32768
N_DP = 32
N_TENSOR = 4


def moment_pair(key, shape):
    first = jax.random.normal(jax.random.fold_in(key, 1), shape, jnp.float32)
    second = jnp.exp(jax.random.uniform(jax.random.fold_in(key, 2), shape, jnp.float32, math.log(0.25), math.log(4.0)))
    return jnp.stack([first, second])


def draw_qk_gain(key, part):
    key = jax.random.fold_in(key, 7)
    return jax.random.uniform(key, (2, HEAD), jnp.float32, 0.5, 1.5)


def draw_q_moments(key, part):
    key = jax.random.fold_in(key, 11)
    return moment_pair(key, (D, HEADS * HEAD))


def draw_kv_moments(key, part):
    key = jax.random.fold_in(key, 13)
    return moment_pair(key, (2, D, KV_HEADS * HEAD))


def draw_o_moments(key, part):
    key = jax.random.fold_in(key, 17)
    return moment_pair(key, (D, HEADS * HEAD))


def levels(key, shape, shards, least, high):
    factor_of, own = 1.0, jax.random.fold_in(key, 6)
    for position, parts in shards:
        steps = jnp.exp(jax.random.uniform(jax.random.fold_in(own, position), (parts,), jnp.float32, least / len(shards), high / len(shards)))
        factor_of = factor_of * jnp.repeat(steps, shape[position] // parts).reshape([-1 if axis == position else 1 for axis in range(len(shape))])
    return factor_of


def split_up(count, total, reach, slope):
    portions = [(1 << 20) // math.isqrt(rank ** slope) + 1 for rank in range(2, count + 1)]
    rest, given = total - reach - (count - 1), [1] * (count - 1)
    while rest > 0:
        candidates = [i for i in range(count - 1) if given[i] < reach]
        whole, left = sum([portions[i] for i in candidates]), rest
        for i in candidates:
            more = min(reach - given[i], max(1, left * portions[i] // whole), rest)
            given[i] = given[i] + more
            rest = rest - more
    return np.array([reach] + given)


def uneven(rng, number_of, total, most, slope):
    if number_of == 2:
        one = jax.random.randint(rng, (), max(1, total - most), min(most, total - 1) + 1)
        return jnp.stack([one, total - one])
    sizes = jnp.asarray(split_up(number_of, total, most, slope), jnp.int32)
    couples = (number_of - 1) // 2
    source_of, receiver = sizes[1:1 + 2 * couples:2], sizes[2:2 + 2 * couples:2]
    slack = jnp.minimum(source_of - 1, most - receiver)
    moved = jax.random.randint(jax.random.fold_in(rng, 1), (couples,), 0, 1 << 20) % (slack + 1)
    sizes = sizes.at[1:1 + 2 * couples:2].set(source_of - moved).at[2:2 + 2 * couples:2].set(receiver + moved)
    return sizes[jax.random.permutation(jax.random.fold_in(rng, 2), number_of)]


def centred(key, shape, deviation, limit, split=(), kind=jnp.bfloat16):
    drawn = jax.random.normal(key, shape, jnp.float32) * deviation
    if len(split) > 0:
        drawn = levels(key, shape, split, -0.22, 0.18) * drawn
    return jnp.clip(drawn, min=-limit, max=limit).astype(kind)


def setup_inputs(seed: int = 0) -> dict:
    streams_of = jax.random.split(jax.random.key(seed), 14)
    return {
        "states": centred(streams_of[0], (TOKENS, D), 1.0, 6.0, ((0, 128),)),
        "lengths": jax.vmap(lambda own: uneven(own, SEQ_GROUP, TOK_GROUP, TOK_GROUP // 2, 2))(jax.random.split(streams_of[1], GROUPS)).reshape((GROUPS, SEQ_GROUP)).astype(jnp.int32),
        "norm_gain": jnp.clip(1.0 + 0.1 * jax.random.normal(streams_of[2], (D,), jnp.float32), 0.5, 1.5),
        "qk_gain": draw_qk_gain(jax.random.fold_in(streams_of[13], 71), 0),
        "q_master": centred(streams_of[4], (D, HEADS * HEAD), D ** -0.5, 0.078125, ((0, 32), (1, 4)), jnp.float32),
        "q_grad": centred(streams_of[5], (D, HEADS * HEAD), 1.0, 6.0, ((0, 32), (1, 4))),
        "q_moments": draw_q_moments(jax.random.fold_in(streams_of[13], 71), 0),
        "kv_master": centred(streams_of[7], (2, D, KV_HEADS * HEAD), D ** -0.5, 0.078125, ((1, 32), (2, 4)), jnp.float32),
        "kv_grad": centred(streams_of[8], (2, D, KV_HEADS * HEAD), 1.0, 6.0, ((1, 32), (2, 4))),
        "kv_moments": draw_kv_moments(jax.random.fold_in(streams_of[13], 71), 0),
        "o_master": centred(streams_of[10], (D, HEADS * HEAD), (HEADS * HEAD) ** -0.5, 0.09375, ((0, 32), (1, 4)), jnp.float32),
        "o_grad": centred(streams_of[11], (D, HEADS * HEAD), 1.0, 6.0, ((0, 32), (1, 4))),
        "o_moments": draw_o_moments(jax.random.fold_in(streams_of[13], 71), 0),
    }


beta_one = 0.9
beta_two = 0.95
adam_eps = 1e-08
learn_rate = 0.001
decay_rate = 0.1
step_count = 100.0
norm_eps = 1e-06
rope_base = 1000000.0

def adam_update(master, grad, moments):
    grad_full = grad.astype(jnp.float32)
    first = beta_one * moments[0] + (1.0 - beta_one) * grad_full
    second = beta_two * moments[1] + (1.0 - beta_two) * grad_full * grad_full
    ratio = first / (1.0 - beta_one ** step_count) / (jnp.sqrt(second / (1.0 - beta_two ** step_count)) + adam_eps)
    updated = master - learn_rate * (ratio + decay_rate * master)
    return (updated, jnp.stack([first, second]))

def rounded(value):
    return lax.optimization_barrier(value.astype(jnp.bfloat16))

def positions_of(lengths_row, count):
    index = jnp.arange(count, dtype=jnp.int32)
    bounds = jnp.cumsum(lengths_row).astype(jnp.int32)
    passed = (index[:, None] >= bounds[None, :]).astype(jnp.int32)
    segment = lax.optimization_barrier(jnp.sum(passed, axis=1)).astype(jnp.int32)
    offset = (index - lax.optimization_barrier(jnp.sum(passed * lengths_row[None, :], axis=1))).astype(jnp.int32)
    return (segment, offset)

def head_norm(values, gain):
    return values * lax.rsqrt(lax.optimization_barrier(jnp.mean(values * values, axis=-1, keepdims=True)) + norm_eps) * gain

def rotate(values, offset):
    half = values.shape[-1] // 2
    freq = rope_base ** (-jnp.arange(half, dtype=jnp.float32) * 2.0 / values.shape[-1])
    angle = offset.astype(jnp.float32)[:, None] * freq[None, :]
    cosine = jnp.cos(angle)[:, None, :]
    sine = jnp.sin(angle)[:, None, :]
    first = values[..., :half]
    second = values[..., half:]
    return jnp.concatenate([first * cosine - second * sine, second * cosine + first * sine], axis=-1)

def score_group(state_rows, lengths_row, norm_gain, qk_gain, q_weight, kv_weight, o_weight):
    count = state_rows.shape[0]
    state_full = state_rows.astype(jnp.float32)
    normed = (state_full * lax.rsqrt(lax.optimization_barrier(jnp.mean(state_full * state_full, axis=-1, keepdims=True)) + norm_eps) * norm_gain).astype(jnp.bfloat16)
    segment, offset = positions_of(lengths_row, count)
    queries = jnp.dot(normed, q_weight, preferred_element_type=jnp.float32).reshape(count, HEADS, HEAD)
    queries = rounded(rotate(head_norm(queries, qk_gain[0]), offset))
    keys = jnp.dot(normed, kv_weight[0], preferred_element_type=jnp.float32).reshape(count, KV_HEADS, HEAD)
    keys = rounded(rotate(head_norm(keys, qk_gain[1]), offset))
    values = rounded(jnp.dot(normed, kv_weight[1], preferred_element_type=jnp.float32)).reshape(count, KV_HEADS, HEAD)
    grouped = queries.reshape(count, KV_HEADS, HEADS // KV_HEADS, HEAD)
    scores = jnp.einsum('bkrh,ckh->krbc', grouped.astype(jnp.float32), keys.astype(jnp.float32)) * HEAD ** (-0.5)
    index = jnp.arange(count, dtype=jnp.int32)
    allowed = (segment[:, None] == segment[None, :]) & (index[None, :] <= index[:, None])
    scores = jnp.where(allowed, scores, -1e+30)
    peak = lax.optimization_barrier(jnp.max(scores, axis=-1, keepdims=True))
    raised = jnp.exp(scores - peak)
    weights = rounded(raised / lax.optimization_barrier(jnp.sum(raised, axis=-1, keepdims=True)))
    context = rounded(jnp.einsum('krbc,ckh->bkrh', weights.astype(jnp.float32), values.astype(jnp.float32)))
    context = context.reshape(count, HEADS * HEAD)
    width = HEADS * HEAD // N_TENSOR
    total = jnp.zeros((count, D), jnp.float32)
    for set_index in range(N_TENSOR):
        low = set_index * width
        piece = lax.dot_general(context[:, low:low + width], o_weight[:, low:low + width], (((1,), (1,)), ((), ())), preferred_element_type=jnp.float32)
        total = total + rounded(piece).astype(jnp.float32)
    return (state_full + total).astype(jnp.bfloat16)

def reference(states, lengths, norm_gain, qk_gain, q_master, q_grad, q_moments, kv_master, kv_grad, kv_moments, o_master, o_grad, o_moments):
    q_new, q_moments_new = adam_update(q_master, q_grad, q_moments)
    kv_new, kv_moments_new = adam_update(kv_master, kv_grad, kv_moments)
    o_new, o_moments_new = adam_update(o_master, o_grad, o_moments)
    q_weight = q_new.astype(jnp.bfloat16)
    kv_weight = kv_new.astype(jnp.bfloat16)
    o_weight = o_new.astype(jnp.bfloat16)
    grouped_rows = states.reshape(N_DP, TOK_GROUP, D)

    def one_group(pair):
        return score_group(pair[0], pair[1], norm_gain, qk_gain, q_weight, kv_weight, o_weight)
    scored = lax.map(one_group, (grouped_rows, lengths)).reshape(TOKENS, D)
    return (scored, q_new, q_moments_new, kv_new, kv_moments_new, o_new, o_moments_new)
```

```python
import jax
import jax.numpy as jnp
from jax import lax
from jax.experimental import pallas as pl
from jax.experimental.pallas import tpu as pltpu
from jax.sharding import PartitionSpec as P

beta_one = 0.9
beta_two = 0.95
adam_eps = 1e-08
learn_rate = 0.001
decay_rate = 0.1
step_count = 100.0
norm_eps = 1e-06
rope_base = 1000000.0

MESH = pl.DeviceIdType.MESH
ROWS = 160
SIDE = 4
BLOCK = 256
CHUNK = 640
STEPS = 8
WIDTHS = (512, 384, 384, 1024)
STARTS = (0, 512, 896)
OUT = 3
NORM_ROWS = 64
NORM_STEPS = BLOCK // NORM_ROWS
WINDOW = 768


def adam_update(master, grad, moments):
    grad_full = grad.astype(jnp.float32)
    first = beta_one * moments[0] + (1.0 - beta_one) * grad_full
    second = beta_two * moments[1] + (1.0 - beta_two) * grad_full * grad_full
    ratio = (
        first
        / (1.0 - beta_one**step_count)
        / (jnp.sqrt(second / (1.0 - beta_two**step_count)) + adam_eps)
    )
    updated = master - learn_rate * (ratio + decay_rate * master)
    return (updated, jnp.stack([first, second]))


def positions_of(lengths_row, count):
    index = jnp.arange(count, dtype=jnp.int32)
    bounds = jnp.cumsum(lengths_row)
    passed = (index[:, None] >= bounds[None, :]).astype(jnp.int32)
    segment = jnp.sum(passed, axis=1)
    offset = index - jnp.sum(passed * lengths_row[None, :], axis=1)
    return (segment, offset)


def layer_kernel(
    weights,
    o_weight,
    states,
    norm_gain,
    qk_gain,
    cosine,
    sine,
    seg_col,
    seg_row,
    scored,
    w0,
    w1,
    w2,
    wo,
    normed,
    rows_in,
    queries,
    keys,
    values,
    context,
    bias,
    sib_far,
    sib_own,
    far_sum,
    local_sem,
    ring_send,
    ring_recv,
    pair_send,
    pair_recv,
    norm_send,
    norm_recv,
    out_send,
    out_recv,
):
    dp = lax.axis_index("dp")
    tensor = lax.axis_index("tensor")
    x, y, z_lo = dp // 8, (dp // 2) % 4, dp % 2
    z_hi, core = tensor // 2, tensor % 2
    units = (w0, w1, w2, wo)

    sibling = (dp, z_hi * 2 + 1 - core)
    across = (dp, (1 - z_hi) * 2 + core)
    pair = (dp + 1 - 2 * z_lo, tensor)

    def wrap(value):
        return lax.rem(value + SIDE, SIDE)

    def plane(px, py):
        return (wrap(px) * 8 + wrap(py) * 2 + z_lo, tensor)

    barrier = pltpu.get_barrier_semaphore()
    partners = (
        plane(x + 1, y),
        plane(x - 1, y),
        plane(x, y + 1),
        plane(x, y - 1),
        pair,
        across,
        sibling,
    )
    for partner in partners:
        pl.semaphore_signal(barrier, inc=1, device_id=partner, device_id_type=MESH)

    def shard(unit, source):
        return units[unit].at[pl.ds(pl.multiple_of(source * ROWS, 32), ROWS), :]

    loads = []
    for unit in range(3):
        loads.append(
            pltpu.make_async_copy(
                weights.at[:, pl.ds(STARTS[unit], WIDTHS[unit])],
                shard(unit, dp),
                local_sem.at[unit],
            )
        )
    loads.append(pltpu.make_async_copy(o_weight, shard(OUT, dp), local_sem.at[OUT]))
    load_rows = pltpu.make_async_copy(states, rows_in, local_sem.at[4])
    loads[0].start()
    load_rows.start()
    for load in loads[1:]:
        load.start()

    pl.semaphore_wait(barrier, len(partners))

    sends = []
    norm_copies = []

    def send(src, dst, send_sem, recv_sem, device, sends=sends):
        copy = pltpu.make_async_remote_copy(
            src_ref=src,
            dst_ref=dst,
            send_sem=send_sem,
            recv_sem=recv_sem,
            device_id=device,
            device_id_type=MESH,
        )
        copy.start()
        sends.append(copy)
        return copy

    def await_recv(dst, recv_sem):
        pltpu.make_async_remote_copy(
            src_ref=dst,
            dst_ref=dst,
            send_sem=pair_send.at[0],
            recv_sem=recv_sem,
            device_id=sibling,
            device_id_type=MESH,
        ).wait_recv()

    def flavour(half):
        return z_lo if half == 0 else 1 - z_lo

    def ring_pos(half):
        turn = flavour(half)
        return (x + turn * (y - x), y + turn * (x - y))

    def ring_place(half, first, second):
        turn = flavour(half)
        first, second = wrap(first), wrap(second)
        return (first + turn * (second - first), second + turn * (first - second))

    def ring_device(half, first, second):
        px, py = ring_place(half, first, second)
        return (px * 8 + py * 2 + z_lo, tensor)

    def ring_shard(unit, half, first, second):
        px, py = ring_place(half, first, second)
        return shard(unit, px * 8 + py * 2 + flavour(half))

    def ring_recv_sem(unit, half, a, b):
        return ring_recv.at[(unit * 2 + half) * 16 + a * 4 + b]

    def ring_send_sem(unit, half, index):
        return ring_send.at[(unit * 2 + half) * 16 + index]

    def pair_start(unit):
        loads[unit].wait()
        send(shard(unit, dp), shard(unit, dp), pair_send.at[unit], pair_recv.at[unit], pair)

    def spread(unit, half, a):
        first, second = ring_pos(half)
        piece = ring_shard(unit, half, first + a, second)
        for index, (step, b) in enumerate(((1, 3), (-1, 1))):
            send(
                piece,
                piece,
                ring_send_sem(unit, half, 3 + 2 * a + index),
                ring_recv_sem(unit, half, a, b),
                ring_device(half, first, second + step),
            )

    def ring_open(unit, half):
        first, second = ring_pos(half)
        piece = ring_shard(unit, half, first, second)
        if half == 1:
            await_recv(piece, pair_recv.at[unit])
        for index, (step, a) in enumerate(((1, 3), (-1, 1))):
            send(
                piece,
                piece,
                ring_send_sem(unit, half, index),
                ring_recv_sem(unit, half, a, 0),
                ring_device(half, first + step, second),
            )
        spread(unit, half, 0)

    def ring_first(unit, half, a):
        first, second = ring_pos(half)
        piece = ring_shard(unit, half, first + a, second)
        await_recv(piece, ring_recv_sem(unit, half, a, 0))
        upward = (half + (unit in (1, 2))) % 2 == 0
        if a == (3 if upward else 1):
            step = 1 if upward else -1
            send(
                piece,
                piece,
                ring_send_sem(unit, half, 2),
                ring_recv_sem(unit, half, 2, 0),
                ring_device(half, first + step, second),
            )
        spread(unit, half, a)

    def ring_second(unit, half, a):
        first, second = ring_pos(half)
        upward = a in (0, 3)
        for b in (1, 3):
            piece = ring_shard(unit, half, first + a, second + b)
            await_recv(piece, ring_recv_sem(unit, half, a, b))
            if b == (3 if upward else 1):
                step = 1 if upward else -1
                send(
                    piece,
                    piece,
                    ring_send_sem(unit, half, 11 + a),
                    ring_recv_sem(unit, half, a, 2),
                    ring_device(half, first, second + step),
                )

    def ring_last(unit, half, a):
        first, second = ring_pos(half)
        piece = ring_shard(unit, half, first + a, second + 2)
        await_recv(piece, ring_recv_sem(unit, half, a, 2))

    def norm_rows(block, step):
        start = pl.multiple_of(block * BLOCK + step * NORM_ROWS, NORM_ROWS)
        return normed.at[pl.ds(start, NORM_ROWS), :]

    def norm_step(step):
        full = rows_in[step * NORM_ROWS : (step + 1) * NORM_ROWS, :].astype(jnp.float32)
        scale = lax.rsqrt(jnp.mean(full * full, axis=-1, keepdims=True) + norm_eps)
        piece = norm_rows(tensor, step)
        piece[...] = (full * scale * norm_gain[...]).astype(jnp.bfloat16)
        send(piece, piece, norm_send.at[step], norm_recv.at[step], across, norm_copies)
        send(piece, piece, norm_send.at[4 + step], norm_recv.at[4 + step], sibling, norm_copies)

    def norm_forward(step):
        piece = norm_rows((1 - z_hi) * 2 + core, step)
        await_recv(piece, norm_recv.at[step])
        send(piece, piece, norm_send.at[8 + step], norm_recv.at[8 + step], sibling, norm_copies)

    def norm_beside(step):
        await_recv(norm_rows(z_hi * 2 + 1 - core, step), norm_recv.at[4 + step])

    def norm_far(step):
        await_recv(norm_rows((1 - z_hi) * 2 + 1 - core, step), norm_recv.at[8 + step])

    def turned(raw, gain, start):
        scale = lax.rsqrt(jnp.mean(raw * raw, axis=-1, keepdims=True) + norm_eps)
        flat = raw * scale * gain
        return (
            flat * cosine[pl.ds(start, BLOCK), :]
            + pltpu.roll(flat, 64, 1) * sine[pl.ds(start, BLOCK), :]
        ).astype(jnp.bfloat16)

    def project(unit, chip, index):
        start = pl.multiple_of(chip * 512 + index * BLOCK, BLOCK)
        raw = jnp.dot(
            normed[pl.ds(start, BLOCK), :], units[unit][...], preferred_element_type=jnp.float32
        )
        for column in range(WIDTHS[unit] // 128):
            part = raw[:, column * 128 : (column + 1) * 128]
            head = STARTS[unit] // 128 + column - 2
            if head == -2:
                keys[pl.ds(start, BLOCK), :] = turned(part, qk_gain[1:2, :], start)
            elif head == -1:
                values[pl.ds(start, BLOCK), :] = part.astype(jnp.bfloat16)
            else:
                queries[head, pl.ds(start, BLOCK), :] = turned(part, qk_gain[0:1, :], start)

    def make_bias(block):
        low = max(block - 2, 0) * BLOCK
        row = block * BLOCK + lax.broadcasted_iota(jnp.int32, (BLOCK, WINDOW), 0)
        column = low + lax.broadcasted_iota(jnp.int32, (BLOCK, WINDOW), 1)
        same = seg_col[block * BLOCK : (block + 1) * BLOCK, :] == seg_row[:, low : low + WINDOW]
        bias[block] = jnp.where(same & (column <= row), 0.0, -1e30)

    def attend(block, first_head, heads):
        start = pl.multiple_of(block * BLOCK, BLOCK)
        low = pl.multiple_of(jnp.maximum(block - 2, 0) * BLOCK, BLOCK)

        def one_head(head, carry):
            scores = lax.dot_general(
                queries[head, pl.ds(start, BLOCK), :],
                keys[pl.ds(low, WINDOW), :],
                (((1,), (1,)), ((), ())),
                preferred_element_type=jnp.float32,
            )
            scores = scores * (128 ** (-0.5)) + bias[block]
            raised = jnp.exp(scores - jnp.max(scores, axis=-1, keepdims=True))
            total = jnp.sum(raised, axis=-1, keepdims=True)
            mixed = jnp.dot(
                raised.astype(jnp.bfloat16),
                values[pl.ds(low, WINDOW), :],
                preferred_element_type=jnp.float32,
            )
            lanes = pl.ds(pl.multiple_of(head * 128, 128), 128)
            context[pl.ds(start, BLOCK), lanes] = (mixed / total).astype(jnp.bfloat16)
            return carry

        lax.fori_loop(first_head, first_head + heads, one_head, 0)

    def chunk_columns(index):
        order = ((0, 0), (0, 1), (1, 0), (1, 1), (3, 0), (3, 1), (2, 0), (2, 1))
        step, half = order[index]
        place = wrap(x + step) * 2 + lax.rem(y // 2 + half, 2)
        return pl.multiple_of(place * CHUNK, 128)

    def out_rows(slot, index):
        return normed.at[slot * BLOCK : (slot + 1) * BLOCK, pl.ds(chunk_columns(index), CHUNK)]

    def column_of(ref, index):
        return ref.at[:, pl.ds(chunk_columns(index), CHUNK)]

    def out_part(chip, slot, index):
        columns = chunk_columns(index)
        for side in range(2):
            block = chip * 2 + (core if side == 0 else 1 - core)
            start = pl.multiple_of(block * BLOCK, BLOCK)
            part = lax.dot_general(
                context[pl.ds(start, BLOCK), :],
                wo[pl.ds(columns, CHUNK), :],
                (((1,), (1,)), ((), ())),
                preferred_element_type=jnp.float32,
            )
            normed[(slot + side) * BLOCK : (slot + side + 1) * BLOCK, pl.ds(columns, CHUNK)] = (
                part.astype(jnp.bfloat16)
            )

    def out_far(index):
        out_part(1 - z_hi, 0, index)
        send(
            out_rows(1, index),
            column_of(sib_far, index),
            out_send.at[index],
            out_recv.at[index],
            sibling,
        )

    def out_far_sum(index):
        await_recv(column_of(sib_far, index), out_recv.at[index])
        piece = out_rows(0, index)
        piece[...] = (
            piece[...].astype(jnp.float32) + column_of(sib_far, index)[...].astype(jnp.float32)
        ).astype(jnp.bfloat16)
        send(
            piece,
            column_of(far_sum, index),
            out_send.at[8 + index],
            out_recv.at[8 + index],
            across,
        )

    def out_own(index):
        out_part(z_hi, 2, index)
        send(
            out_rows(3, index),
            column_of(sib_own, index),
            out_send.at[16 + index],
            out_recv.at[16 + index],
            sibling,
        )

    def out_final(index):
        await_recv(column_of(sib_own, index), out_recv.at[16 + index])
        await_recv(column_of(far_sum, index), out_recv.at[8 + index])
        total = out_rows(2, index)[...].astype(jnp.float32)
        total = total + column_of(sib_own, index)[...].astype(jnp.float32)
        total = total + column_of(far_sum, index)[...].astype(jnp.float32)
        total = total + column_of(rows_in, index)[...].astype(jnp.float32)
        column_of(scored, index)[...] = total.astype(jnp.bfloat16)

    def both(step, unit, *rest):
        for half in range(2):
            step(unit, half, *rest)

    pair_start(0)
    ring_open(0, 0)
    load_rows.wait()
    norm_step(0)
    pair_start(1)
    norm_step(1)
    ring_open(0, 1)
    norm_step(2)
    pair_start(2)
    norm_step(3)
    pair_start(3)
    for a in (1, 3, 2):
        both(ring_first, 0, a)
    both(ring_open, 1)
    for block in range(4):
        make_bias(block)
    for a, b in ((0, 1), (1, 3), (3, 2), (2, None)):
        both(ring_second, 0, a)
        if b is not None:
            both(ring_first, 1, b)
    norm_forward(0)
    both(ring_open, 2)
    for a in range(4):
        both(ring_last, 0, a)
    for step in range(NORM_STEPS):
        norm_beside(step)
    both(ring_second, 1, 0)
    project(0, z_hi, 0)
    both(ring_first, 2, 1)
    both(ring_second, 1, 1)
    project(0, z_hi, 1)
    norm_forward(1)
    both(ring_first, 2, 3)
    both(ring_second, 1, 3)
    both(ring_first, 2, 2)
    both(ring_second, 1, 2)
    norm_forward(2)
    both(ring_open, OUT)
    for a in range(4):
        both(ring_last, 1, a)
    both(ring_second, 2, 0)
    project(1, z_hi, 0)
    both(ring_first, OUT, 1)
    both(ring_second, 2, 1)
    project(1, z_hi, 1)
    both(ring_first, OUT, 3)
    both(ring_second, 2, 3)
    both(ring_first, OUT, 2)
    both(ring_second, 2, 2)
    norm_forward(3)
    for a in range(4):
        both(ring_last, 2, a)
    project(2, z_hi, 0)
    project(2, z_hi, 1)
    for step in range(NORM_STEPS):
        norm_far(step)
    both(ring_second, OUT, 0)
    for unit in range(3):
        project(unit, 1 - z_hi, 0)
        project(unit, 1 - z_hi, 1)
    both(ring_second, OUT, 1)
    attend((1 - z_hi) * 2, 0, 4)
    attend((1 - z_hi) * 2, 4, 4)
    both(ring_second, OUT, 3)
    attend((1 - z_hi) * 2 + 1, 0, 4)
    attend((1 - z_hi) * 2 + 1, 4, 4)
    both(ring_second, OUT, 2)
    for a in range(4):
        both(ring_last, OUT, a)
    for copy in norm_copies:
        copy.wait_send()
    for index in range(STEPS):
        out_far(index)
        if index > 0:
            out_far_sum(index - 1)
    out_far_sum(STEPS - 1)
    for block in range(2):
        attend(z_hi * 2 + block, 0, 8)
    for index in range(STEPS):
        out_own(index)
    for index in range(STEPS):
        out_final(index)
    for copy in sends:
        copy.wait_send()


def layer(weights, o_weight, states, norm_gain, qk_gain, cosine, sine, seg_col, seg_row):
    bf16, f32 = jnp.bfloat16, jnp.float32
    width = states.shape[1]
    tokens = seg_col.shape[0]
    vmem = pl.BlockSpec(memory_space=pltpu.VMEM)
    hbm = pl.BlockSpec(memory_space=pl.ANY)
    return pl.pallas_call(
        layer_kernel,
        out_shape=jax.ShapeDtypeStruct(states.shape, bf16),
        in_specs=[hbm, hbm, hbm] + [vmem] * 6,
        out_specs=vmem,
        scratch_shapes=[
            *[pltpu.VMEM((width, columns), bf16) for columns in WIDTHS],
            pltpu.VMEM((tokens, width), bf16),
            pltpu.VMEM((BLOCK, width), bf16),
            pltpu.VMEM((8, tokens, 128), bf16),
            pltpu.VMEM((tokens, 128), bf16),
            pltpu.VMEM((tokens, 128), bf16),
            pltpu.VMEM((tokens, 1024), bf16),
            pltpu.VMEM((4, BLOCK, WINDOW), f32),
            pltpu.VMEM((BLOCK, width), bf16),
            pltpu.VMEM((BLOCK, width), bf16),
            pltpu.VMEM((BLOCK, width), bf16),
            pltpu.SemaphoreType.DMA((5,)),
            pltpu.SemaphoreType.DMA((128,)),
            pltpu.SemaphoreType.DMA((128,)),
            pltpu.SemaphoreType.DMA((4,)),
            pltpu.SemaphoreType.DMA((4,)),
            pltpu.SemaphoreType.DMA((12,)),
            pltpu.SemaphoreType.DMA((12,)),
            pltpu.SemaphoreType.DMA((24,)),
            pltpu.SemaphoreType.DMA((24,)),
        ],
        compiler_params=pltpu.CompilerParams(
            collective_id=1, has_side_effects=True, vmem_limit_bytes=62 * 2**20
        ),
        cost_estimate=pl.CostEstimate(
            flops=30_000_000_000, bytes_accessed=10_000_000, transcendentals=5_000_000
        ),
        name="layer",
    )(weights, o_weight, states, norm_gain, qk_gain, cosine, sine, seg_col, seg_row)


def per_device(
    states,
    lengths,
    norm_gain,
    qk_gain,
    q_master,
    q_grad,
    q_moments,
    kv_master,
    kv_grad,
    kv_moments,
    o_master,
    o_grad,
    o_moments,
):
    q_new, q_moments_new = adam_update(q_master, q_grad, q_moments)
    kv_new, kv_moments_new = adam_update(kv_master, kv_grad, kv_moments)
    o_new, o_moments_new = adam_update(o_master, o_grad, o_moments)
    weights = jnp.concatenate([kv_new[0], kv_new[1], q_new], axis=1).astype(jnp.bfloat16)
    count = 1024
    half = qk_gain.shape[1] // 2
    segment, offset = positions_of(lengths[0], count)
    freq = rope_base ** (-jnp.arange(half, dtype=jnp.float32) * 2.0 / qk_gain.shape[1])
    angle = offset.astype(jnp.float32)[:, None] * freq[None, :]
    cosine, sine = jnp.cos(angle), jnp.sin(angle)
    scored = layer(
        weights,
        o_new.astype(jnp.bfloat16),
        states,
        norm_gain[None, :],
        qk_gain,
        jnp.concatenate([cosine, cosine], axis=1),
        jnp.concatenate([-sine, sine], axis=1),
        segment[:, None],
        segment[None, :],
    )
    return (scored, q_new, q_moments_new, kv_new, kv_moments_new, o_new, o_moments_new)


def solution(mesh):
    return jax.shard_map(
        per_device,
        mesh=mesh,
        in_specs=(
            P(("dp", "tensor"), None),
            P("dp", None),
            P(),
            P(),
            P("dp", "tensor"),
            P("dp", "tensor"),
            P(None, "dp", "tensor"),
            P(None, "dp", "tensor"),
            P(None, "dp", "tensor"),
            P(None, None, "dp", "tensor"),
            P("dp", "tensor"),
            P("dp", "tensor"),
            P(None, "dp", "tensor"),
        ),
        out_specs=(
            P(("dp", "tensor"), None),
            P("dp", "tensor"),
            P(None, "dp", "tensor"),
            P(None, "dp", "tensor"),
            P(None, None, "dp", "tensor"),
            P("dp", "tensor"),
            P(None, "dp", "tensor"),
        ),
        check_vma=False,
    )
```

```python
import jax
import jax.numpy as jnp
import numpy as np
from jax import lax
from jax.experimental import pallas as pl
from jax.experimental.pallas import tpu as pltpu
from jax.sharding import PartitionSpec as P

beta_one = 0.9
beta_two = 0.95
adam_eps = 1e-08
learn_rate = 0.001
decay_rate = 0.1
step_count = 100.0
norm_eps = 1e-06
rope_base = 1000000.0

MESH = pl.DeviceIdType.MESH
ROWS = 160
SIDE = 4
BLOCK = 256
CHUNK = 640
STEPS = 8
WIDTHS = (512, 512, 256, 1024)
STARTS = (0, 512, 1024)
OUT = 3
NORM_ROWS = 64
NORM_STEPS = BLOCK // NORM_ROWS
WINDOW = 768


def adam_update(master, grad, first, second):
    grad_full = grad.astype(jnp.float32)
    first = beta_one * first + (1.0 - beta_one) * grad_full
    second = beta_two * second + (1.0 - beta_two) * grad_full * grad_full
    ratio = (
        first
        / (1.0 - beta_one**step_count)
        / (jnp.sqrt(second / (1.0 - beta_two**step_count)) + adam_eps)
    )
    return (master - learn_rate * (ratio + decay_rate * master), first, second)


def adam_kernel(
    q_master,
    q_grad,
    q_moments,
    kv_master,
    kv_grad,
    kv_moments,
    o_master,
    o_grad,
    o_moments,
    q_new,
    q_moments_new,
    kv_new,
    kv_moments_new,
    o_new,
    o_moments_new,
    weights,
    o_weight,
):
    for master, grad, moments, new, moments_new, low in (
        (q_master, q_grad, q_moments, q_new, q_moments_new, weights.at[:, 256:]),
        (o_master, o_grad, o_moments, o_new, o_moments_new, o_weight),
    ):
        updated, first, second = adam_update(master[...], grad[...], moments[0], moments[1])
        new[...] = updated
        moments_new[0] = first
        moments_new[1] = second
        low[...] = updated.astype(jnp.bfloat16)
    for index in range(2):
        updated, first, second = adam_update(
            kv_master[index], kv_grad[index], kv_moments[0, index], kv_moments[1, index]
        )
        kv_new[index] = updated
        kv_moments_new[0, index] = first
        kv_moments_new[1, index] = second
        weights[:, index * 128 : (index + 1) * 128] = updated.astype(jnp.bfloat16)


def adam(*arrays):
    rows = 32
    steps = ROWS // rows

    def spec(shape):
        lead = len(shape) - 2
        return pl.BlockSpec(
            shape[:lead] + (rows, shape[-1]), lambda step: (0,) * lead + (step, 0)
        )

    shapes = [array.shape for array in arrays]
    made = [(shapes[index], jnp.float32) for index in (0, 2, 3, 5, 6, 8)]
    made = made + [((ROWS, 1280), jnp.bfloat16), ((ROWS, 1024), jnp.bfloat16)]
    return pl.pallas_call(
        adam_kernel,
        grid=(steps,),
        out_shape=[jax.ShapeDtypeStruct(shape, kind) for shape, kind in made],
        in_specs=[spec(shape) for shape in shapes],
        out_specs=[spec(shape) for shape, _ in made],
        compiler_params=pltpu.CompilerParams(vmem_limit_bytes=32 * 2**20),
        name="adam",
    )(*arrays)


def layer_kernel(
    weights,
    o_weight,
    states,
    norm_gain,
    qk_gain,
    lengths,
    freq,
    scored,
    w0,
    w1,
    w2,
    wo,
    normed,
    rows_in,
    queries,
    keys,
    values,
    context,
    bias,
    cosine,
    sine,
    sib_far,
    sib_own,
    far_sum,
    local_sem,
    ring_send,
    ring_recv,
    pair_send,
    pair_recv,
    norm_send,
    norm_recv,
    out_send,
    out_recv,
    store_sem,
):
    dp = lax.axis_index("dp")
    tensor = lax.axis_index("tensor")
    x, y, z_lo = dp // 8, (dp // 2) % 4, dp % 2
    z_hi, core = tensor // 2, tensor % 2
    units = (w0, w1, w2, wo)

    sibling = (dp, z_hi * 2 + 1 - core)
    across = (dp, (1 - z_hi) * 2 + core)
    pair = (dp + 1 - 2 * z_lo, tensor)

    def wrap(value):
        return lax.rem(value + SIDE, SIDE)

    def plane(px, py):
        return (wrap(px) * 8 + wrap(py) * 2 + z_lo, tensor)

    barrier = pltpu.get_barrier_semaphore()
    partners = (
        plane(x + 1, y),
        plane(x - 1, y),
        plane(x, y + 1),
        plane(x, y - 1),
        pair,
        across,
        sibling,
    )
    for partner in partners:
        pl.semaphore_signal(barrier, inc=1, device_id=partner, device_id_type=MESH)

    def shard(unit, source):
        return units[unit].at[pl.ds(pl.multiple_of(source * ROWS, 32), ROWS), :]

    loads = []
    for unit in range(3):
        loads.append(
            pltpu.make_async_copy(
                weights.at[:, pl.ds(STARTS[unit], WIDTHS[unit])],
                shard(unit, dp),
                local_sem.at[unit],
            )
        )
    loads.append(pltpu.make_async_copy(o_weight, shard(OUT, dp), local_sem.at[OUT]))
    load_rows = pltpu.make_async_copy(states, rows_in, local_sem.at[4])
    loads[0].start()
    load_rows.start()
    for load in loads[1:]:
        load.start()

    pl.semaphore_wait(barrier, len(partners))

    sends = []
    norm_copies = []
    stores = []

    def send(src, dst, send_sem, recv_sem, device, sends=sends):
        copy = pltpu.make_async_remote_copy(
            src_ref=src,
            dst_ref=dst,
            send_sem=send_sem,
            recv_sem=recv_sem,
            device_id=device,
            device_id_type=MESH,
        )
        copy.start()
        sends.append(copy)
        return copy

    def await_recv(dst, recv_sem):
        pltpu.make_async_remote_copy(
            src_ref=dst,
            dst_ref=dst,
            send_sem=pair_send.at[0],
            recv_sem=recv_sem,
            device_id=sibling,
            device_id_type=MESH,
        ).wait_recv()

    def flavour(half):
        return z_lo if half == 0 else 1 - z_lo

    def ring_pos(half):
        turn = flavour(half)
        return (x + turn * (y - x), y + turn * (x - y))

    def ring_place(half, first, second):
        turn = flavour(half)
        first, second = wrap(first), wrap(second)
        return (first + turn * (second - first), second + turn * (first - second))

    def ring_device(half, first, second):
        px, py = ring_place(half, first, second)
        return (px * 8 + py * 2 + z_lo, tensor)

    def ring_shard(unit, half, first, second):
        px, py = ring_place(half, first, second)
        return shard(unit, px * 8 + py * 2 + flavour(half))

    def ring_recv_sem(unit, half, a, b):
        return ring_recv.at[(unit * 2 + half) * 16 + a * 4 + b]

    def ring_send_sem(unit, half, index):
        return ring_send.at[(unit * 2 + half) * 16 + index]

    def pair_start(unit):
        loads[unit].wait()
        send(shard(unit, dp), shard(unit, dp), pair_send.at[unit], pair_recv.at[unit], pair)

    def spread(unit, half, a):
        first, second = ring_pos(half)
        piece = ring_shard(unit, half, first + a, second)
        for index, (step, b) in enumerate(((1, 3), (-1, 1))):
            send(
                piece,
                piece,
                ring_send_sem(unit, half, 3 + 2 * a + index),
                ring_recv_sem(unit, half, a, b),
                ring_device(half, first, second + step),
            )

    def ring_open(unit, half):
        first, second = ring_pos(half)
        piece = ring_shard(unit, half, first, second)
        if half == 1:
            await_recv(piece, pair_recv.at[unit])
        for index, (step, a) in enumerate(((1, 3), (-1, 1))):
            send(
                piece,
                piece,
                ring_send_sem(unit, half, index),
                ring_recv_sem(unit, half, a, 0),
                ring_device(half, first + step, second),
            )
        spread(unit, half, 0)

    def ring_first(unit, half, a):
        first, second = ring_pos(half)
        piece = ring_shard(unit, half, first + a, second)
        await_recv(piece, ring_recv_sem(unit, half, a, 0))
        upward = (half + (unit in (1, 2))) % 2 == 0
        if a == (3 if upward else 1):
            step = 1 if upward else -1
            send(
                piece,
                piece,
                ring_send_sem(unit, half, 2),
                ring_recv_sem(unit, half, 2, 0),
                ring_device(half, first + step, second),
            )
        spread(unit, half, a)

    def ring_second(unit, half, a):
        first, second = ring_pos(half)
        upward = a in (0, 3)
        for b in (1, 3):
            piece = ring_shard(unit, half, first + a, second + b)
            await_recv(piece, ring_recv_sem(unit, half, a, b))
            if b == (3 if upward else 1):
                step = 1 if upward else -1
                send(
                    piece,
                    piece,
                    ring_send_sem(unit, half, 11 + a),
                    ring_recv_sem(unit, half, a, 2),
                    ring_device(half, first, second + step),
                )

    def ring_last(unit, half, a):
        first, second = ring_pos(half)
        piece = ring_shard(unit, half, first + a, second + 2)
        await_recv(piece, ring_recv_sem(unit, half, a, 2))

    def turn_last(unit, turn, a):
        half = z_lo if turn == 0 else 1 - z_lo
        px, py = (wrap(x + a), wrap(y + 2)) if turn == 0 else (wrap(x + 2), wrap(y + a))
        await_recv(shard(unit, px * 8 + py * 2 + turn), ring_recv_sem(unit, half, a, 2))

    def norm_rows(block, step):
        start = pl.multiple_of(block * BLOCK + step * NORM_ROWS, NORM_ROWS)
        return normed.at[pl.ds(start, NORM_ROWS), :]

    def norm_step(step):
        full = rows_in[step * NORM_ROWS : (step + 1) * NORM_ROWS, :].astype(jnp.float32)
        scale = lax.rsqrt(jnp.mean(full * full, axis=-1, keepdims=True) + norm_eps)
        piece = norm_rows(tensor, step)
        piece[...] = (full * scale * norm_gain[...]).astype(jnp.bfloat16)
        send(piece, piece, norm_send.at[step], norm_recv.at[step], across, norm_copies)
        send(piece, piece, norm_send.at[4 + step], norm_recv.at[4 + step], sibling, norm_copies)

    def norm_forward(step):
        piece = norm_rows((1 - z_hi) * 2 + core, step)
        await_recv(piece, norm_recv.at[step])
        send(piece, piece, norm_send.at[8 + step], norm_recv.at[8 + step], sibling, norm_copies)

    def norm_beside(step):
        await_recv(norm_rows(z_hi * 2 + 1 - core, step), norm_recv.at[4 + step])

    def norm_far(step):
        await_recv(norm_rows((1 - z_hi) * 2 + 1 - core, step), norm_recv.at[8 + step])

    def turned(raw, gain, start, rows):
        scale = lax.rsqrt(jnp.mean(raw * raw, axis=-1, keepdims=True) + norm_eps)
        flat = raw * scale * gain
        return (
            flat * cosine[pl.ds(start, rows), :]
            + pltpu.roll(flat, 64, 1) * sine[pl.ds(start, rows), :]
        ).astype(jnp.bfloat16)

    def project(unit, chip, offset, rows):
        start = pl.multiple_of(chip * 512 + offset, 128)
        raw = jnp.dot(
            normed[pl.ds(start, rows), :], units[unit][...], preferred_element_type=jnp.float32
        )
        for column in range(WIDTHS[unit] // 128):
            part = raw[:, column * 128 : (column + 1) * 128]
            head = STARTS[unit] // 128 + column - 2
            if head == -2:
                keys[pl.ds(start, rows), :] = turned(part, qk_gain[1:2, :], start, rows)
            elif head == -1:
                values[pl.ds(start, rows), :] = part.astype(jnp.bfloat16)
            else:
                queries[head, pl.ds(start, rows), :] = turned(part, qk_gain[0:1, :], start, rows)

    def begin_of(row):
        begin, bound = jnp.zeros_like(row), 0
        for index in range(8):
            bound = bound + lengths[0, index]
            begin = jnp.where(row >= bound, bound, begin)
        return begin

    def make_tables(block):
        row = block * BLOCK + lax.broadcasted_iota(jnp.int32, (BLOCK, 128), 0)
        angle = (row - begin_of(row)).astype(jnp.float32) * freq[...]
        lane = lax.broadcasted_iota(jnp.int32, (BLOCK, 128), 1)
        rows = slice(block * BLOCK, (block + 1) * BLOCK)
        cosine[rows, :] = jnp.cos(angle)
        sine[rows, :] = jnp.where(lane < 64, -1.0, 1.0) * jnp.sin(angle)

    def make_bias(block):
        low = max(block - 2, 0) * BLOCK
        row = block * BLOCK + lax.broadcasted_iota(jnp.int32, (BLOCK, 1), 0)
        column = low + lax.broadcasted_iota(jnp.int32, (BLOCK, WINDOW), 1)
        bias[block] = jnp.where((column >= begin_of(row)) & (column <= row), 0.0, -1e30)

    def attend(block, first_head, heads):
        start = pl.multiple_of(block * BLOCK, BLOCK)
        low = pl.multiple_of(jnp.maximum(block - 2, 0) * BLOCK, BLOCK)

        def one_head(head, carry):
            scores = lax.dot_general(
                queries[head, pl.ds(start, BLOCK), :],
                keys[pl.ds(low, WINDOW), :],
                (((1,), (1,)), ((), ())),
                preferred_element_type=jnp.float32,
            )
            scores = scores * (128 ** (-0.5)) + bias[block]
            raised = jnp.exp(scores - jnp.max(scores, axis=-1, keepdims=True))
            total = jnp.sum(raised, axis=-1, keepdims=True)
            mixed = jnp.dot(
                raised.astype(jnp.bfloat16),
                values[pl.ds(low, WINDOW), :],
                preferred_element_type=jnp.float32,
            )
            lanes = pl.ds(pl.multiple_of(head * 128, 128), 128)
            context[pl.ds(start, BLOCK), lanes] = (mixed / total).astype(jnp.bfloat16)
            return carry

        lax.fori_loop(first_head, first_head + heads, one_head, 0)

    def chunk_columns(index):
        order = ((0, 0), (0, 1), (1, 0), (1, 1), (3, 0), (3, 1), (2, 0), (2, 1))
        step, half = order[index]
        place = wrap(x + step) * 2 + lax.rem(y // 2 + half, 2)
        return pl.multiple_of(place * CHUNK, 128)

    def out_rows(slot, index):
        return normed.at[slot * BLOCK : (slot + 1) * BLOCK, pl.ds(chunk_columns(index), CHUNK)]

    def column_of(ref, index):
        return ref.at[:, pl.ds(chunk_columns(index), CHUNK)]

    def out_part(chip, slot, index):
        columns = chunk_columns(index)
        for side in range(2):
            block = chip * 2 + (core if side == 0 else 1 - core)
            start = pl.multiple_of(block * BLOCK, BLOCK)
            part = lax.dot_general(
                context[pl.ds(start, BLOCK), :],
                wo[pl.ds(columns, CHUNK), :],
                (((1,), (1,)), ((), ())),
                preferred_element_type=jnp.float32,
            )
            normed[(slot + side) * BLOCK : (slot + side + 1) * BLOCK, pl.ds(columns, CHUNK)] = (
                part.astype(jnp.bfloat16)
            )

    def out_far(index):
        out_part(1 - z_hi, 0, index)
        send(
            out_rows(1, index),
            column_of(sib_far, index),
            out_send.at[index],
            out_recv.at[index],
            sibling,
        )

    def out_far_sum(index):
        await_recv(column_of(sib_far, index), out_recv.at[index])
        piece = out_rows(0, index)
        piece[...] = (
            piece[...].astype(jnp.float32) + column_of(sib_far, index)[...].astype(jnp.float32)
        ).astype(jnp.bfloat16)
        send(
            piece,
            column_of(far_sum, index),
            out_send.at[8 + index],
            out_recv.at[8 + index],
            across,
        )

    def out_own(index):
        out_part(z_hi, 2, index)
        send(
            out_rows(3, index),
            column_of(sib_own, index),
            out_send.at[16 + index],
            out_recv.at[16 + index],
            sibling,
        )

    def out_final(index):
        await_recv(column_of(sib_own, index), out_recv.at[16 + index])
        await_recv(column_of(far_sum, index), out_recv.at[8 + index])
        total = out_rows(2, index)[...].astype(jnp.float32)
        total = total + column_of(sib_own, index)[...].astype(jnp.float32)
        total = total + column_of(far_sum, index)[...].astype(jnp.float32)
        total = total + column_of(rows_in, index)[...].astype(jnp.float32)
        column_of(rows_in, index)[...] = total.astype(jnp.bfloat16)
        copy = pltpu.make_async_copy(
            column_of(rows_in, index), column_of(scored, index), store_sem.at[index]
        )
        copy.start()
        stores.append(copy)

    def both(step, unit, *rest):
        for half in range(2):
            step(unit, half, *rest)

    near, far = z_hi, 1 - z_hi
    pair_start(0)
    ring_open(0, 0)
    load_rows.wait()
    norm_step(0)
    norm_step(1)
    ring_open(0, 1)
    pair_start(1)
    norm_step(2)
    norm_step(3)
    pair_start(2)
    for a in (1, 3, 2):
        both(ring_first, 0, a)
    both(ring_open, 1)
    for a, b in ((0, 1), (1, 3), (3, 2), (2, None)):
        make_tables(a)
        both(ring_second, 0, a)
        if b is not None:
            both(ring_first, 1, b)
    norm_forward(0)
    both(ring_open, 2)
    make_bias(0)
    make_bias(1)
    for a in range(4):
        both(ring_last, 0, a)
    for step in range(NORM_STEPS):
        norm_beside(step)
    both(ring_second, 1, 0)
    project(0, near, 0, 256)
    both(ring_first, 2, 1)
    both(ring_second, 1, 1)
    project(0, near, 256, 256)
    norm_forward(1)
    both(ring_first, 2, 3)
    both(ring_second, 1, 3)
    make_bias(2)
    make_bias(3)
    both(ring_first, 2, 2)
    both(ring_second, 1, 2)
    norm_far(0)
    norm_far(1)
    project(0, far, 0, 128)
    project(0, far, 256, 128)
    norm_forward(2)
    pair_start(OUT)
    for a in range(4):
        both(ring_last, 1, a)
    both(ring_second, 2, 0)
    project(1, near, 0, 256)
    both(ring_second, 2, 1)
    project(1, near, 256, 256)
    both(ring_second, 2, 3)
    project(1, far, 0, 128)
    project(1, far, 256, 128)
    both(ring_second, 2, 2)
    norm_forward(3)
    both(ring_open, OUT)
    for a in range(4):
        both(ring_last, 2, a)
    project(2, near, 0, 256)
    project(2, near, 256, 256)
    norm_far(2)
    norm_far(3)
    project(0, far, 128, 128)
    project(0, far, 384, 128)
    both(ring_first, OUT, 1)
    project(1, far, 128, 128)
    project(1, far, 384, 128)
    both(ring_first, OUT, 3)
    project(2, far, 0, 256)
    project(2, far, 256, 256)
    both(ring_first, OUT, 2)
    attend(far * 2, 0, 8)
    both(ring_second, OUT, 0)
    attend(far * 2 + 1, 0, 8)
    for copy in norm_copies:
        copy.wait_send()
    turn_last(OUT, 0, 0)
    out_far(0)
    out_far(1)
    out_far_sum(0)
    out_far_sum(1)
    both(ring_second, OUT, 1)
    attend(near * 2, 0, 4)
    both(ring_second, OUT, 3)
    attend(near * 2, 4, 4)
    both(ring_second, OUT, 2)
    turn_last(OUT, 0, 1)
    turn_last(OUT, 0, 3)
    for index in (2, 3, 4, 5):
        out_far(index)
        if index > 2:
            out_far_sum(index - 1)
    out_far_sum(5)
    attend(near * 2 + 1, 0, 8)
    for index in range(2):
        out_own(index)
    turn_last(OUT, 0, 2)
    for a in range(4):
        turn_last(OUT, 1, a)
    out_far(6)
    out_far(7)
    out_far_sum(6)
    out_far_sum(7)
    for index in range(2, STEPS):
        out_own(index)
    for index in range(STEPS):
        out_final(index)
    for copy in sends:
        copy.wait_send()
    for copy in stores:
        copy.wait()


def layer(weights, o_weight, states, norm_gain, qk_gain, lengths, freq):
    bf16, f32 = jnp.bfloat16, jnp.float32
    width = states.shape[1]
    tokens = 4 * BLOCK
    vmem = pl.BlockSpec(memory_space=pltpu.VMEM)
    hbm = pl.BlockSpec(memory_space=pl.ANY)
    return pl.pallas_call(
        layer_kernel,
        out_shape=jax.ShapeDtypeStruct(states.shape, bf16),
        in_specs=[hbm, hbm, hbm, vmem, vmem, pl.BlockSpec(memory_space=pltpu.SMEM), vmem],
        out_specs=hbm,
        scratch_shapes=[
            *[pltpu.VMEM((width, columns), bf16) for columns in WIDTHS],
            pltpu.VMEM((tokens, width), bf16),
            pltpu.VMEM((BLOCK, width), bf16),
            pltpu.VMEM((8, tokens, 128), bf16),
            pltpu.VMEM((tokens, 128), bf16),
            pltpu.VMEM((tokens, 128), bf16),
            pltpu.VMEM((tokens, 1024), bf16),
            pltpu.VMEM((4, BLOCK, WINDOW), f32),
            pltpu.VMEM((tokens, 128), f32),
            pltpu.VMEM((tokens, 128), f32),
            pltpu.VMEM((BLOCK, width), bf16),
            pltpu.VMEM((BLOCK, width), bf16),
            pltpu.VMEM((BLOCK, width), bf16),
            pltpu.SemaphoreType.DMA((5,)),
            pltpu.SemaphoreType.DMA((128,)),
            pltpu.SemaphoreType.DMA((128,)),
            pltpu.SemaphoreType.DMA((4,)),
            pltpu.SemaphoreType.DMA((4,)),
            pltpu.SemaphoreType.DMA((12,)),
            pltpu.SemaphoreType.DMA((12,)),
            pltpu.SemaphoreType.DMA((24,)),
            pltpu.SemaphoreType.DMA((24,)),
            pltpu.SemaphoreType.DMA((STEPS,)),
        ],
        compiler_params=pltpu.CompilerParams(
            collective_id=1, has_side_effects=True, vmem_limit_bytes=62 * 2**20
        ),
        cost_estimate=pl.CostEstimate(
            flops=30_000_000_000, bytes_accessed=10_000_000, transcendentals=5_000_000
        ),
        name="layer",
    )(weights, o_weight, states, norm_gain, qk_gain, lengths, freq)


def per_device(
    states,
    lengths,
    norm_gain,
    qk_gain,
    q_master,
    q_grad,
    q_moments,
    kv_master,
    kv_grad,
    kv_moments,
    o_master,
    o_grad,
    o_moments,
):
    q_new, q_moments_new, kv_new, kv_moments_new, o_new, o_moments_new, weights, o_weight = adam(
        q_master,
        q_grad,
        q_moments,
        kv_master,
        kv_grad,
        kv_moments,
        o_master,
        o_grad,
        o_moments,
    )
    head = qk_gain.shape[1]
    half = np.arange(head // 2) * 2.0 / head
    freq = np.tile(rope_base**-half, 2)[None, :].astype(np.float32)
    scored = layer(
        weights, o_weight, states, norm_gain[None, :], qk_gain, lengths, jnp.asarray(freq)
    )
    return (scored, q_new, q_moments_new, kv_new, kv_moments_new, o_new, o_moments_new)


def solution(mesh):
    return jax.shard_map(
        per_device,
        mesh=mesh,
        in_specs=(
            P(("dp", "tensor"), None),
            P("dp", None),
            P(),
            P(),
            P("dp", "tensor"),
            P("dp", "tensor"),
            P(None, "dp", "tensor"),
            P(None, "dp", "tensor"),
            P(None, "dp", "tensor"),
            P(None, None, "dp", "tensor"),
            P("dp", "tensor"),
            P("dp", "tensor"),
            P(None, "dp", "tensor"),
        ),
        out_specs=(
            P(("dp", "tensor"), None),
            P("dp", "tensor"),
            P(None, "dp", "tensor"),
            P(None, "dp", "tensor"),
            P(None, None, "dp", "tensor"),
            P("dp", "tensor"),
            P(None, "dp", "tensor"),
        ),
        check_vma=False,
    )
```

```python
import jax
import jax.numpy as jnp
import numpy as np
from jax import lax
from jax.experimental import pallas as pl
from jax.experimental.pallas import tpu as pltpu
from jax.sharding import PartitionSpec as P

beta_one = 0.9
beta_two = 0.95
adam_eps = 1e-08
learn_rate = 0.001
decay_rate = 0.1
step_count = 100.0
norm_eps = 1e-06
rope_base = 1000000.0
LOG2_E = 1.4426950408889634

MESH = pl.DeviceIdType.MESH
ROWS = 160
SIDE = 4
BLOCK = 256
CHUNK = 640
STEPS = 8
WIDTHS = (512, 512, 256, 1024)
STARTS = (0, 512, 1024)
OUT = 3
NORM_ROWS = 64
NORM_STEPS = BLOCK // NORM_ROWS
WINDOW = 768


def adam_update(master, grad, first, second):
    grad_full = grad.astype(jnp.float32)
    first = beta_one * first + (1.0 - beta_one) * grad_full
    second = beta_two * second + (1.0 - beta_two) * grad_full * grad_full
    ratio = (
        first
        / (1.0 - beta_one**step_count)
        / (jnp.sqrt(second / (1.0 - beta_two**step_count)) + adam_eps)
    )
    return (master - learn_rate * (ratio + decay_rate * master), first, second)


def adam_kernel(
    q_master,
    q_grad,
    q_moments,
    kv_master,
    kv_grad,
    kv_moments,
    o_master,
    o_grad,
    o_moments,
    q_new,
    q_moments_new,
    kv_new,
    kv_moments_new,
    o_new,
    o_moments_new,
    weights,
    o_weight,
):
    for master, grad, moments, new, moments_new, low in (
        (q_master, q_grad, q_moments, q_new, q_moments_new, weights.at[:, 256:]),
        (o_master, o_grad, o_moments, o_new, o_moments_new, o_weight),
    ):
        updated, first, second = adam_update(master[...], grad[...], moments[0], moments[1])
        new[...] = updated
        moments_new[0] = first
        moments_new[1] = second
        low[...] = updated.astype(jnp.bfloat16)
    for index in range(2):
        updated, first, second = adam_update(
            kv_master[index], kv_grad[index], kv_moments[0, index], kv_moments[1, index]
        )
        kv_new[index] = updated
        kv_moments_new[0, index] = first
        kv_moments_new[1, index] = second
        weights[:, index * 128 : (index + 1) * 128] = updated.astype(jnp.bfloat16)


def adam(*arrays):
    rows = 32
    steps = ROWS // rows

    def spec(shape):
        lead = len(shape) - 2
        return pl.BlockSpec(
            shape[:lead] + (rows, shape[-1]), lambda step: (0,) * lead + (step, 0)
        )

    shapes = [array.shape for array in arrays]
    made = [(shapes[index], jnp.float32) for index in (0, 2, 3, 5, 6, 8)]
    made = made + [((ROWS, 1280), jnp.bfloat16), ((ROWS, 1024), jnp.bfloat16)]
    return pl.pallas_call(
        adam_kernel,
        grid=(steps,),
        out_shape=[jax.ShapeDtypeStruct(shape, kind) for shape, kind in made],
        in_specs=[spec(shape) for shape in shapes],
        out_specs=[spec(shape) for shape, _ in made],
        compiler_params=pltpu.CompilerParams(vmem_limit_bytes=62 * 2**20),
        name="adam",
    )(*arrays)


def layer_kernel(
    weights,
    o_weight,
    states,
    norm_gain,
    qk_gain,
    lengths,
    freq,
    scored,
    w0,
    w1,
    w2,
    wo,
    normed,
    rows_in,
    queries,
    keys,
    values,
    context,
    bias,
    cosine,
    sine,
    far_parts,
    sib_far,
    sib_own,
    far_sum,
    local_sem,
    ring_send,
    ring_recv,
    pair_send,
    pair_recv,
    norm_send,
    norm_recv,
    out_send,
    out_recv,
    store_sem,
):
    dp = lax.axis_index("dp")
    tensor = lax.axis_index("tensor")
    x, y, z_lo = dp // 8, (dp // 2) % 4, dp % 2
    z_hi, core = tensor // 2, tensor % 2
    near, far = z_hi, 1 - z_hi
    units = (w0, w1, w2, wo)

    sibling = (dp, z_hi * 2 + 1 - core)
    across = (dp, (1 - z_hi) * 2 + core)
    pair = (dp + 1 - 2 * z_lo, tensor)

    def wrap(value):
        return lax.rem(value + SIDE, SIDE)

    def plane(px, py):
        return (wrap(px) * 8 + wrap(py) * 2 + z_lo, tensor)

    barrier = pltpu.get_barrier_semaphore()
    partners = (
        plane(x + 1, y),
        plane(x - 1, y),
        plane(x, y + 1),
        plane(x, y - 1),
        pair,
        across,
        (dp, (1 - z_hi) * 2 + 1 - core),
        sibling,
    )
    for partner in partners:
        pl.semaphore_signal(barrier, inc=1, device_id=partner, device_id_type=MESH)

    def shard(unit, source):
        return units[unit].at[pl.ds(pl.multiple_of(source * ROWS, 32), ROWS), :]

    loads = []
    for unit in range(3):
        loads.append(
            pltpu.make_async_copy(
                weights.at[:, pl.ds(STARTS[unit], WIDTHS[unit])],
                shard(unit, dp),
                local_sem.at[unit],
            )
        )
    loads.append(pltpu.make_async_copy(o_weight, shard(OUT, dp), local_sem.at[OUT]))
    load_rows = pltpu.make_async_copy(states, rows_in, local_sem.at[4])
    loads[0].start()
    load_rows.start()
    for load in loads[1:]:
        load.start()

    pl.semaphore_wait(barrier, len(partners))

    sends = []
    norm_copies = []
    stores = []

    def send(src, dst, send_sem, recv_sem, device, sends=sends):
        copy = pltpu.make_async_remote_copy(
            src_ref=src,
            dst_ref=dst,
            send_sem=send_sem,
            recv_sem=recv_sem,
            device_id=device,
            device_id_type=MESH,
        )
        copy.start()
        sends.append(copy)
        return copy

    def await_recv(dst, recv_sem):
        pltpu.make_async_remote_copy(
            src_ref=dst,
            dst_ref=dst,
            send_sem=pair_send.at[0],
            recv_sem=recv_sem,
            device_id=sibling,
            device_id_type=MESH,
        ).wait_recv()

    def flavour(half):
        return z_lo if half == 0 else 1 - z_lo

    def ring_pos(half):
        turn = flavour(half)
        return (x + turn * (y - x), y + turn * (x - y))

    def ring_place(half, first, second):
        turn = flavour(half)
        first, second = wrap(first), wrap(second)
        return (first + turn * (second - first), second + turn * (first - second))

    def ring_device(half, first, second):
        px, py = ring_place(half, first, second)
        return (px * 8 + py * 2 + z_lo, tensor)

    def ring_shard(unit, half, first, second):
        px, py = ring_place(half, first, second)
        return shard(unit, px * 8 + py * 2 + flavour(half))

    def ring_recv_sem(unit, half, a, b):
        return ring_recv.at[(unit * 2 + half) * 16 + a * 4 + b]

    def ring_send_sem(unit, half, index):
        return ring_send.at[(unit * 2 + half) * 16 + index]

    def pair_start(unit):
        loads[unit].wait()
        send(shard(unit, dp), shard(unit, dp), pair_send.at[unit], pair_recv.at[unit], pair)

    def spread(unit, half, a):
        first, second = ring_pos(half)
        piece = ring_shard(unit, half, first + a, second)
        for index, (step, b) in enumerate(((1, 3), (-1, 1))):
            send(
                piece,
                piece,
                ring_send_sem(unit, half, 3 + 2 * a + index),
                ring_recv_sem(unit, half, a, b),
                ring_device(half, first, second + step),
            )

    def ring_open(unit, half):
        first, second = ring_pos(half)
        piece = ring_shard(unit, half, first, second)
        if half == 1:
            await_recv(piece, pair_recv.at[unit])
        for index, (step, a) in enumerate(((1, 3), (-1, 1))):
            send(
                piece,
                piece,
                ring_send_sem(unit, half, index),
                ring_recv_sem(unit, half, a, 0),
                ring_device(half, first + step, second),
            )
        spread(unit, half, 0)

    def ring_head(unit, half, a):
        first, second = ring_pos(half)
        piece = ring_shard(unit, half, first + a, second)
        await_recv(piece, ring_recv_sem(unit, half, a, 0))
        upward = (half + (unit in (1, 2))) % 2 == 0
        if a == (3 if upward else 1):
            step = 1 if upward else -1
            send(
                piece,
                piece,
                ring_send_sem(unit, half, 2),
                ring_recv_sem(unit, half, 2, 0),
                ring_device(half, first + step, second),
            )

    def ring_first(unit, half, a):
        ring_head(unit, half, a)
        spread(unit, half, a)

    def ring_second(unit, half, a):
        first, second = ring_pos(half)
        upward = a in (0, 3)
        for b in (1, 3):
            piece = ring_shard(unit, half, first + a, second + b)
            await_recv(piece, ring_recv_sem(unit, half, a, b))
            if b == (3 if upward else 1):
                step = 1 if upward else -1
                send(
                    piece,
                    piece,
                    ring_send_sem(unit, half, 11 + a),
                    ring_recv_sem(unit, half, a, 2),
                    ring_device(half, first, second + step),
                )

    def ring_last(unit, half, a):
        first, second = ring_pos(half)
        piece = ring_shard(unit, half, first + a, second + 2)
        await_recv(piece, ring_recv_sem(unit, half, a, 2))

    def turn_last(unit, turn, a):
        half = z_lo if turn == 0 else 1 - z_lo
        px, py = (wrap(x + a), wrap(y + 2)) if turn == 0 else (wrap(x + 2), wrap(y + a))
        await_recv(shard(unit, px * 8 + py * 2 + turn), ring_recv_sem(unit, half, a, 2))

    def norm_rows(block, step):
        start = pl.multiple_of(block * BLOCK + step * NORM_ROWS, NORM_ROWS)
        return normed.at[pl.ds(start, NORM_ROWS), :]

    def norm_step(step):
        full = rows_in[step * NORM_ROWS : (step + 1) * NORM_ROWS, :].astype(jnp.float32)
        scale = lax.rsqrt(jnp.mean(full * full, axis=-1, keepdims=True) + norm_eps)
        piece = norm_rows(tensor, step)
        piece[...] = (full * scale * norm_gain[...]).astype(jnp.bfloat16)
        send(piece, piece, norm_send.at[4 + step], norm_recv.at[4 + step], sibling, norm_copies)

    def norm_beside(step):
        await_recv(norm_rows(z_hi * 2 + 1 - core, step), norm_recv.at[4 + step])

    def half_rows(chip, step, side):
        start = pl.multiple_of(chip * 512 + step * 128 + side * 64, 64)
        return normed.at[pl.ds(start, 64), :]

    def norm_across(step):
        piece = half_rows(near, step, core)
        send(piece, piece, norm_send.at[step], norm_recv.at[step], across, norm_copies)

    def norm_forward(step):
        piece = half_rows(far, step, core)
        await_recv(piece, norm_recv.at[step])
        send(piece, piece, norm_send.at[8 + step], norm_recv.at[8 + step], sibling, norm_copies)

    def norm_far(step):
        await_recv(half_rows(far, step, 1 - core), norm_recv.at[8 + step])

    def turned(raw, gain, start, rows):
        scale = lax.rsqrt(jnp.mean(raw * raw, axis=-1, keepdims=True) + norm_eps)
        flat = raw * scale * gain
        return (
            flat * cosine[pl.ds(start, rows), :]
            + pltpu.roll(flat, 64, 1) * sine[pl.ds(start, rows), :]
        ).astype(jnp.bfloat16)

    def project(unit, chip, offset, rows):
        start = pl.multiple_of(chip * 512 + offset, 128)
        raw = jnp.dot(
            normed[pl.ds(start, rows), :], units[unit][...], preferred_element_type=jnp.float32
        )
        for column in range(WIDTHS[unit] // 128):
            part = raw[:, column * 128 : (column + 1) * 128]
            head = STARTS[unit] // 128 + column - 2
            if head == -2:
                keys[pl.ds(start, rows), :] = turned(part, qk_gain[1:2, :], start, rows)
            elif head == -1:
                values[pl.ds(start, rows), :] = part.astype(jnp.bfloat16)
            else:
                queries[head, pl.ds(start, rows), :] = turned(part, qk_gain[0:1, :], start, rows)

    def begin_of(row):
        begin, bound = jnp.zeros_like(row), 0
        for index in range(8):
            bound = bound + lengths[0, index]
            begin = jnp.where(row >= bound, bound, begin)
        return begin

    def make_tables(block):
        row = block * BLOCK + lax.broadcasted_iota(jnp.int32, (BLOCK, 128), 0)
        angle = (row - begin_of(row)).astype(jnp.float32) * freq[...]
        lane = lax.broadcasted_iota(jnp.int32, (BLOCK, 128), 1)
        rows = slice(block * BLOCK, (block + 1) * BLOCK)
        cosine[rows, :] = jnp.cos(angle)
        sine[rows, :] = jnp.where(lane < 64, -1.0, 1.0) * jnp.sin(angle)

    def make_bias(block):
        low = max(block - 2, 0) * BLOCK
        row = block * BLOCK + lax.broadcasted_iota(jnp.int32, (BLOCK, 1), 0)
        column = low + lax.broadcasted_iota(jnp.int32, (BLOCK, WINDOW), 1)
        bias[block] = jnp.where((column >= begin_of(row)) & (column <= row), 0.0, -1e30)

    def attend(block, first_head, heads):
        start = pl.multiple_of(block * BLOCK, BLOCK)
        low = pl.multiple_of(jnp.maximum(block - 2, 0) * BLOCK, BLOCK)

        def two_heads(index, carry):
            head = first_head + 2 * index
            pair_of = queries[pl.ds(head, 2), pl.ds(start, BLOCK), :].reshape(2 * BLOCK, 128)
            scores = lax.dot_general(
                pair_of,
                keys[pl.ds(low, WINDOW), :],
                (((1,), (1,)), ((), ())),
                preferred_element_type=jnp.float32,
            ).reshape(2, BLOCK, WINDOW)
            scores = scores * (128 ** (-0.5) * LOG2_E) + bias[block][None]
            raised = jnp.exp2(scores - jnp.max(scores, axis=-1, keepdims=True))
            total = jnp.sum(raised, axis=-1, keepdims=True)
            mixed = jnp.dot(
                raised.astype(jnp.bfloat16).reshape(2 * BLOCK, WINDOW),
                values[pl.ds(low, WINDOW), :],
                preferred_element_type=jnp.float32,
            ).reshape(2, BLOCK, 128)
            mixed = (mixed / total).astype(jnp.bfloat16)
            for side in range(2):
                lanes = pl.ds(pl.multiple_of((head + side) * 128, 128), 128)
                context[pl.ds(start, BLOCK), lanes] = mixed[side]
            return carry

        lax.fori_loop(0, heads // 2, two_heads, 0)

    own_mine, own_other = normed.at[0:BLOCK, :], normed.at[BLOCK : 2 * BLOCK, :]

    def chunk_columns(index):
        order = ((0, 0), (0, 1), (1, 0), (1, 1), (3, 0), (3, 1), (2, 0), (2, 1))
        step, half = order[index]
        place = wrap(x + step) * 2 + lax.rem(y // 2 + half, 2)
        return pl.multiple_of(place * CHUNK, 128)

    def column_of(ref, index):
        return ref.at[:, pl.ds(chunk_columns(index), CHUNK)]

    def out_part(block, target, index):
        start = pl.multiple_of(block * BLOCK, BLOCK)
        part = lax.dot_general(
            context[pl.ds(start, BLOCK), :],
            wo[pl.ds(chunk_columns(index), CHUNK), :],
            (((1,), (1,)), ((), ())),
            preferred_element_type=jnp.float32,
        )
        column_of(target, index)[...] = part.astype(jnp.bfloat16)

    def far_half(block, side):
        return far_parts.at[pl.ds(pl.multiple_of(block * BLOCK + side * 128, 128), 128), :]

    def sib_half(block):
        return sib_far.at[block * 128 : (block + 1) * 128, :]

    def out_far(index, block):
        out_part(far * 2 + block, far_parts.at[block * BLOCK : (block + 1) * BLOCK, :], index)
        send(
            column_of(far_half(block, 1 - core), index),
            column_of(sib_half(block), index),
            out_send.at[index * 2 + block],
            out_recv.at[index * 2 + block],
            sibling,
        )

    def sum_half(side):
        return far_sum.at[pl.ds(pl.multiple_of(side * 128, 128), 128), :]

    def out_far_sum(index, block):
        await_recv(column_of(sib_half(block), index), out_recv.at[index * 2 + block])
        piece = column_of(far_half(block, core), index)
        piece[...] = (
            piece[...].astype(jnp.float32)
            + column_of(sib_half(block), index)[...].astype(jnp.float32)
        ).astype(jnp.bfloat16)
        send(
            piece,
            column_of(sum_half(core), index),
            out_send.at[16 + index * 2 + block],
            out_recv.at[16 + index * 2 + core],
            (dp, far * 2 + block),
        )

    def out_own(index):
        out_part(near * 2 + 1 - core, own_other, index)
        out_part(near * 2 + core, own_mine, index)
        send(
            column_of(own_other, index),
            column_of(sib_own, index),
            out_send.at[32 + index],
            out_recv.at[32 + index],
            sibling,
        )

    def out_final(index):
        await_recv(column_of(sib_own, index), out_recv.at[32 + index])
        for side in range(2):
            await_recv(column_of(sum_half(side), index), out_recv.at[16 + index * 2 + side])
        total = column_of(own_mine, index)[...].astype(jnp.float32)
        total = total + column_of(sib_own, index)[...].astype(jnp.float32)
        total = total + column_of(far_sum, index)[...].astype(jnp.float32)
        total = total + column_of(rows_in, index)[...].astype(jnp.float32)
        column_of(rows_in, index)[...] = total.astype(jnp.bfloat16)
        copy = pltpu.make_async_copy(
            column_of(rows_in, index), column_of(scored, index), store_sem.at[index]
        )
        copy.start()
        stores.append(copy)

    def both(step, unit, *rest):
        for half in range(2):
            step(unit, half, *rest)

    pair_start(0)
    ring_open(0, 0)
    load_rows.wait()
    for step in range(NORM_STEPS):
        norm_step(step)
    ring_open(0, 1)
    pair_start(1)
    pair_start(2)
    for step in range(NORM_STEPS):
        norm_beside(step)
    norm_across(0)
    both(ring_first, 0, 1)
    both(ring_first, 0, 3)
    norm_across(1)
    both(ring_first, 0, 2)
    both(ring_open, 1)
    both(ring_second, 0, 0)
    both(ring_first, 1, 1)
    pair_start(OUT)
    norm_across(2)
    make_tables(0)
    make_bias(0)
    both(ring_second, 0, 1)
    both(ring_first, 1, 3)
    make_tables(1)
    make_bias(1)
    both(ring_second, 0, 3)
    both(ring_first, 1, 2)
    norm_across(3)
    make_tables(2)
    make_bias(2)
    both(ring_second, 0, 2)
    both(ring_open, 2)
    make_tables(3)
    make_bias(3)
    norm_forward(0)
    for a in range(4):
        both(ring_last, 0, a)
    both(ring_second, 1, 0)
    both(ring_first, 2, 1)
    project(0, near, 0, 256)
    both(ring_second, 1, 1)
    both(ring_first, 2, 3)
    project(0, near, 256, 256)
    both(ring_second, 1, 3)
    both(ring_first, 2, 2)
    norm_forward(1)
    both(ring_second, 1, 2)
    norm_far(0)
    norm_far(1)
    project(0, far, 0, 256)
    for a in range(4):
        both(ring_last, 1, a)
    both(ring_second, 2, 0)
    project(1, near, 0, 256)
    both(ring_second, 2, 1)
    both(ring_second, 2, 3)
    both(ring_second, 2, 2)
    ring_open(OUT, 0)
    project(1, near, 256, 256)
    project(1, far, 0, 256)
    ring_open(OUT, 1)
    norm_forward(2)
    attend(far * 2, 0, 6)
    for a in range(4):
        both(ring_last, 2, a)
    ring_head(OUT, 0, 1)
    ring_head(OUT, 0, 3)
    project(2, far, 0, 256)
    ring_head(OUT, 1, 1)
    ring_head(OUT, 1, 3)
    attend(far * 2, 6, 2)
    norm_forward(3)
    both(ring_second, OUT, 0)
    both(spread, OUT, 1)
    norm_far(2)
    norm_far(3)
    project(0, far, 256, 256)
    project(1, far, 256, 256)
    both(spread, OUT, 3)
    turn_last(OUT, 0, 0)
    both(ring_head, OUT, 2)
    out_far(0, 0)
    out_far(1, 0)
    out_far_sum(0, 0)
    project(2, far, 256, 256)
    out_far_sum(1, 0)
    attend(far * 2 + 1, 0, 8)
    both(ring_second, OUT, 1)
    both(spread, OUT, 2)
    out_far(0, 1)
    out_far(1, 1)
    out_far_sum(0, 1)
    out_far_sum(1, 1)
    project(2, near, 0, 256)
    project(2, near, 256, 256)
    both(ring_second, OUT, 3)
    attend(near * 2, 0, 4)
    turn_last(OUT, 0, 1)
    both(ring_second, OUT, 2)
    turn_last(OUT, 0, 3)
    for index in (2, 3, 4, 5):
        for block in range(2):
            out_far(index, block)
        for block in range(2):
            out_far_sum(index, block)
    attend(near * 2, 4, 4)
    attend(near * 2 + 1, 0, 8)
    turn_last(OUT, 0, 2)
    for a in range(4):
        turn_last(OUT, 1, a)
    for index in (6, 7):
        for block in range(2):
            out_far(index, block)
        for block in range(2):
            out_far_sum(index, block)
    for copy in norm_copies:
        copy.wait_send()
    for index in range(STEPS):
        out_own(index)
    for index in range(STEPS):
        out_final(index)
    for copy in sends:
        copy.wait_send()
    for copy in stores:
        copy.wait()


def layer(weights, o_weight, states, norm_gain, qk_gain, lengths, freq):
    bf16, f32 = jnp.bfloat16, jnp.float32
    width = states.shape[1]
    tokens = 4 * BLOCK
    vmem = pl.BlockSpec(memory_space=pltpu.VMEM)
    hbm = pl.BlockSpec(memory_space=pl.ANY)
    return pl.pallas_call(
        layer_kernel,
        out_shape=jax.ShapeDtypeStruct(states.shape, bf16),
        in_specs=[hbm, hbm, hbm, vmem, vmem, pl.BlockSpec(memory_space=pltpu.SMEM), vmem],
        out_specs=hbm,
        scratch_shapes=[
            *[pltpu.VMEM((width, columns), bf16) for columns in WIDTHS],
            pltpu.VMEM((tokens, width), bf16),
            pltpu.VMEM((BLOCK, width), bf16),
            pltpu.VMEM((8, tokens, 128), bf16),
            pltpu.VMEM((tokens, 128), bf16),
            pltpu.VMEM((tokens, 128), bf16),
            pltpu.VMEM((tokens, 1024), bf16),
            pltpu.VMEM((4, BLOCK, WINDOW), f32),
            pltpu.VMEM((tokens, 128), f32),
            pltpu.VMEM((tokens, 128), f32),
            pltpu.VMEM((2 * BLOCK, width), bf16),
            *[pltpu.VMEM((BLOCK, width), bf16) for _ in range(3)],
            pltpu.SemaphoreType.DMA((5,)),
            pltpu.SemaphoreType.DMA((128,)),
            pltpu.SemaphoreType.DMA((128,)),
            pltpu.SemaphoreType.DMA((4,)),
            pltpu.SemaphoreType.DMA((4,)),
            pltpu.SemaphoreType.DMA((12,)),
            pltpu.SemaphoreType.DMA((12,)),
            pltpu.SemaphoreType.DMA((40,)),
            pltpu.SemaphoreType.DMA((40,)),
            pltpu.SemaphoreType.DMA((STEPS,)),
        ],
        compiler_params=pltpu.CompilerParams(
            collective_id=1, has_side_effects=True, vmem_limit_bytes=62 * 2**20
        ),
        cost_estimate=pl.CostEstimate(
            flops=30_000_000_000, bytes_accessed=10_000_000, transcendentals=5_000_000
        ),
        name="layer",
    )(weights, o_weight, states, norm_gain, qk_gain, lengths, freq)


def per_device(
    states,
    lengths,
    norm_gain,
    qk_gain,
    q_master,
    q_grad,
    q_moments,
    kv_master,
    kv_grad,
    kv_moments,
    o_master,
    o_grad,
    o_moments,
):
    q_new, q_moments_new, kv_new, kv_moments_new, o_new, o_moments_new, weights, o_weight = adam(
        q_master,
        q_grad,
        q_moments,
        kv_master,
        kv_grad,
        kv_moments,
        o_master,
        o_grad,
        o_moments,
    )
    head = qk_gain.shape[1]
    half = np.arange(head // 2) * 2.0 / head
    freq = np.tile(rope_base**-half, 2)[None, :].astype(np.float32)
    scored = layer(
        weights, o_weight, states, norm_gain[None, :], qk_gain, lengths, jnp.asarray(freq)
    )
    return (scored, q_new, q_moments_new, kv_new, kv_moments_new, o_new, o_moments_new)


def solution(mesh):
    return jax.shard_map(
        per_device,
        mesh=mesh,
        in_specs=(
            P(("dp", "tensor"), None),
            P("dp", None),
            P(),
            P(),
            P("dp", "tensor"),
            P("dp", "tensor"),
            P(None, "dp", "tensor"),
            P(None, "dp", "tensor"),
            P(None, "dp", "tensor"),
            P(None, None, "dp", "tensor"),
            P("dp", "tensor"),
            P("dp", "tensor"),
            P(None, "dp", "tensor"),
        ),
        out_specs=(
            P(("dp", "tensor"), None),
            P("dp", "tensor"),
            P(None, "dp", "tensor"),
            P(None, "dp", "tensor"),
            P(None, None, "dp", "tensor"),
            P("dp", "tensor"),
            P(None, "dp", "tensor"),
        ),
        check_vma=False,
    )
```

```python
import jax
import jax.numpy as jnp
import numpy as np
from jax import lax
from jax.experimental import pallas as pl
from jax.experimental.pallas import tpu as pltpu
from jax.sharding import PartitionSpec as P

beta_one = 0.9
beta_two = 0.95
adam_eps = 1e-08
learn_rate = 0.001
decay_rate = 0.1
step_count = 100.0
norm_eps = 1e-06
rope_base = 1000000.0
LOG2_E = 1.4426950408889634

MESH = pl.DeviceIdType.MESH
ROWS = 160
SIDE = 4
BLOCK = 256
CHUNK = 640
STEPS = 8
WIDTHS = (512, 512, 256, 1024)
STARTS = (0, 512, 1024)
OUT = 3
NORM_ROWS = 64
NORM_STEPS = BLOCK // NORM_ROWS
WINDOW = 768


def adam_update(master, grad, first, second):
    grad_full = grad.astype(jnp.float32)
    first = beta_one * first + (1.0 - beta_one) * grad_full
    second = beta_two * second + (1.0 - beta_two) * grad_full * grad_full
    ratio = (
        first
        / (1.0 - beta_one**step_count)
        / (jnp.sqrt(second / (1.0 - beta_two**step_count)) + adam_eps)
    )
    return (master - learn_rate * (ratio + decay_rate * master), first, second)


def adam_kernel(
    q_master,
    q_grad,
    q_moments,
    kv_master,
    kv_grad,
    kv_moments,
    o_master,
    o_grad,
    o_moments,
    q_new,
    q_moments_new,
    kv_new,
    kv_moments_new,
    o_new,
    o_moments_new,
    weights,
    o_weight,
):
    for master, grad, moments, new, moments_new, low in (
        (q_master, q_grad, q_moments, q_new, q_moments_new, weights.at[:, 256:]),
        (o_master, o_grad, o_moments, o_new, o_moments_new, o_weight),
    ):
        updated, first, second = adam_update(master[...], grad[...], moments[0], moments[1])
        new[...] = updated
        moments_new[0] = first
        moments_new[1] = second
        low[...] = updated.astype(jnp.bfloat16)
    for index in range(2):
        updated, first, second = adam_update(
            kv_master[index], kv_grad[index], kv_moments[0, index], kv_moments[1, index]
        )
        kv_new[index] = updated
        kv_moments_new[0, index] = first
        kv_moments_new[1, index] = second
        weights[:, index * 128 : (index + 1) * 128] = updated.astype(jnp.bfloat16)


def adam(*arrays):
    rows = 80
    steps = ROWS // rows

    def spec(shape):
        lead = len(shape) - 2
        return pl.BlockSpec(
            shape[:lead] + (rows, shape[-1]), lambda step: (0,) * lead + (step, 0)
        )

    shapes = [array.shape for array in arrays]
    made = [(shapes[index], jnp.float32) for index in (0, 2, 3, 5, 6, 8)]
    made = made + [((ROWS, 1280), jnp.bfloat16), ((ROWS, 1024), jnp.bfloat16)]
    return pl.pallas_call(
        adam_kernel,
        grid=(steps,),
        out_shape=[jax.ShapeDtypeStruct(shape, kind) for shape, kind in made],
        in_specs=[spec(shape) for shape in shapes],
        out_specs=[spec(shape) for shape, _ in made],
        compiler_params=pltpu.CompilerParams(vmem_limit_bytes=62 * 2**20),
        name="adam",
    )(*arrays)


def layer_kernel(
    weights,
    o_weight,
    states,
    norm_gain,
    qk_gain,
    lengths,
    freq,
    scored,
    w0,
    w1,
    w2,
    wo,
    normed,
    rows_in,
    queries,
    keys,
    values,
    context,
    bias,
    cosine,
    sine,
    far_parts,
    sib_far,
    sib_own,
    far_sum,
    local_sem,
    ring_send,
    ring_recv,
    pair_send,
    pair_recv,
    norm_send,
    norm_recv,
    out_send,
    out_recv,
    store_sem,
):
    dp = lax.axis_index("dp")
    tensor = lax.axis_index("tensor")
    x, y, z_lo = dp // 8, (dp // 2) % 4, dp % 2
    z_hi, core = tensor // 2, tensor % 2
    near, far = z_hi, 1 - z_hi
    units = (w0, w1, w2, wo)

    sibling = (dp, z_hi * 2 + 1 - core)
    across = (dp, (1 - z_hi) * 2 + core)
    pair = (dp + 1 - 2 * z_lo, tensor)

    def wrap(value):
        return lax.rem(value + SIDE, SIDE)

    def plane(px, py):
        return (wrap(px) * 8 + wrap(py) * 2 + z_lo, tensor)

    barrier = pltpu.get_barrier_semaphore()
    partners = (
        plane(x + 1, y),
        plane(x - 1, y),
        plane(x, y + 1),
        plane(x, y - 1),
        pair,
        across,
        (dp, (1 - z_hi) * 2 + 1 - core),
        sibling,
    )
    for partner in partners:
        pl.semaphore_signal(barrier, inc=1, device_id=partner, device_id_type=MESH)

    def shard(unit, source):
        return units[unit].at[pl.ds(pl.multiple_of(source * ROWS, 32), ROWS), :]

    loads = []
    for unit in range(3):
        loads.append(
            pltpu.make_async_copy(
                weights.at[:, pl.ds(STARTS[unit], WIDTHS[unit])],
                shard(unit, dp),
                local_sem.at[unit],
            )
        )
    loads.append(pltpu.make_async_copy(o_weight, shard(OUT, dp), local_sem.at[OUT]))
    load_rows = pltpu.make_async_copy(states, rows_in, local_sem.at[4])
    loads[0].start()
    load_rows.start()
    for load in loads[1:]:
        load.start()

    pl.semaphore_wait(barrier, len(partners))

    sends = []
    norm_copies = []
    stores = []

    def send(src, dst, send_sem, recv_sem, device, sends=sends):
        copy = pltpu.make_async_remote_copy(
            src_ref=src,
            dst_ref=dst,
            send_sem=send_sem,
            recv_sem=recv_sem,
            device_id=device,
            device_id_type=MESH,
        )
        copy.start()
        sends.append(copy)
        return copy

    def await_recv(dst, recv_sem):
        pltpu.make_async_remote_copy(
            src_ref=dst,
            dst_ref=dst,
            send_sem=pair_send.at[0],
            recv_sem=recv_sem,
            device_id=sibling,
            device_id_type=MESH,
        ).wait_recv()

    def flavour(half):
        return z_lo + half * (1 - 2 * z_lo)

    def ring_pos(half):
        turn = flavour(half)
        return (x + turn * (y - x), y + turn * (x - y))

    def ring_place(half, first, second):
        turn = flavour(half)
        first, second = wrap(first), wrap(second)
        return (first + turn * (second - first), second + turn * (first - second))

    def ring_device(half, first, second):
        px, py = ring_place(half, first, second)
        return (px * 8 + py * 2 + z_lo, tensor)

    def ring_shard(unit, half, first, second):
        px, py = ring_place(half, first, second)
        return shard(unit, px * 8 + py * 2 + flavour(half))

    def ring_recv_sem(unit, half, a, b):
        return ring_recv.at[(unit * 2 + half) * 16 + a * 4 + b]

    def ring_send_sem(unit, half, index):
        return ring_send.at[(unit * 2 + half) * 16 + index]

    def pair_start(unit):
        loads[unit].wait()
        send(shard(unit, dp), shard(unit, dp), pair_send.at[unit], pair_recv.at[unit], pair)

    def spread(unit, half, a):
        first, second = ring_pos(half)
        piece = ring_shard(unit, half, first + a, second)
        for index, (step, b) in enumerate(((1, 3), (-1, 1))):
            send(
                piece,
                piece,
                ring_send_sem(unit, half, 3 + 2 * a + index),
                ring_recv_sem(unit, half, a, b),
                ring_device(half, first, second + step),
            )

    def ring_open(unit, half):
        first, second = ring_pos(half)
        piece = ring_shard(unit, half, first, second)
        if half == 1:
            await_recv(piece, pair_recv.at[unit])
        for index, (step, a) in enumerate(((1, 3), (-1, 1))):
            send(
                piece,
                piece,
                ring_send_sem(unit, half, index),
                ring_recv_sem(unit, half, a, 0),
                ring_device(half, first + step, second),
            )
        spread(unit, half, 0)

    def ring_head(unit, half, a):
        first, second = ring_pos(half)
        piece = ring_shard(unit, half, first + a, second)
        await_recv(piece, ring_recv_sem(unit, half, a, 0))
        upward = (half + (unit in (1, 2))) % 2 == 0
        if a == (3 if upward else 1):
            step = 1 if upward else -1
            send(
                piece,
                piece,
                ring_send_sem(unit, half, 2),
                ring_recv_sem(unit, half, 2, 0),
                ring_device(half, first + step, second),
            )

    def ring_first(unit, half, a):
        ring_head(unit, half, a)
        spread(unit, half, a)

    def ring_second(unit, half, a, upward=None):
        first, second = ring_pos(half)
        upward = a in (0, 3) if upward is None else upward
        for b in (1, 3):
            piece = ring_shard(unit, half, first + a, second + b)
            await_recv(piece, ring_recv_sem(unit, half, a, b))
            if b == (3 if upward else 1):
                step = 1 if upward else -1
                send(
                    piece,
                    piece,
                    ring_send_sem(unit, half, 11 + a),
                    ring_recv_sem(unit, half, a, 2),
                    ring_device(half, first, second + step),
                )

    def ring_last(unit, half, a):
        first, second = ring_pos(half)
        piece = ring_shard(unit, half, first + a, second + 2)
        await_recv(piece, ring_recv_sem(unit, half, a, 2))

    def half_of(turn):
        return turn + z_lo * (1 - 2 * turn)

    def turn_last(unit, turn, a):
        half = half_of(turn)
        px, py = (wrap(x + a), wrap(y + 2)) if turn == 0 else (wrap(x + 2), wrap(y + a))
        await_recv(shard(unit, px * 8 + py * 2 + turn), ring_recv_sem(unit, half, a, 2))

    def norm_rows(block, step):
        start = pl.multiple_of(block * BLOCK + step * NORM_ROWS, NORM_ROWS)
        return normed.at[pl.ds(start, NORM_ROWS), :]

    def norm_step(step):
        full = rows_in[step * NORM_ROWS : (step + 1) * NORM_ROWS, :].astype(jnp.float32)
        scale = lax.rsqrt(jnp.mean(full * full, axis=-1, keepdims=True) + norm_eps)
        piece = norm_rows(tensor, step)
        piece[...] = (full * scale * norm_gain[...]).astype(jnp.bfloat16)
        send(piece, piece, norm_send.at[4 + step], norm_recv.at[4 + step], sibling, norm_copies)

    def norm_beside(step):
        await_recv(norm_rows(z_hi * 2 + 1 - core, step), norm_recv.at[4 + step])

    def half_rows(chip, step, side):
        start = pl.multiple_of(chip * 512 + step * 128 + side * 64, 64)
        return normed.at[pl.ds(start, 64), :]

    def norm_across(step):
        piece = half_rows(near, step, core)
        send(piece, piece, norm_send.at[step], norm_recv.at[step], across, norm_copies)

    def norm_forward(step):
        piece = half_rows(far, step, core)
        await_recv(piece, norm_recv.at[step])
        send(piece, piece, norm_send.at[8 + step], norm_recv.at[8 + step], sibling, norm_copies)

    def norm_far(step):
        await_recv(half_rows(far, step, 1 - core), norm_recv.at[8 + step])

    def turned(raw, gain, start, rows):
        scale = lax.rsqrt(jnp.mean(raw * raw, axis=-1, keepdims=True) + norm_eps)
        flat = raw * scale * gain
        return (
            flat * cosine[pl.ds(start, rows), :]
            + pltpu.roll(flat, 64, 1) * sine[pl.ds(start, rows), :]
        ).astype(jnp.bfloat16)

    def project(unit, chip, offset, rows):
        start = pl.multiple_of(chip * 512 + offset, 128)
        raw = jnp.dot(
            normed[pl.ds(start, rows), :], units[unit][...], preferred_element_type=jnp.float32
        )
        for column in range(WIDTHS[unit] // 128):
            part = raw[:, column * 128 : (column + 1) * 128]
            head = STARTS[unit] // 128 + column - 2
            if head == -2:
                keys[pl.ds(start, rows), :] = turned(part, qk_gain[1:2, :], start, rows)
            elif head == -1:
                values[pl.ds(start, rows), :] = part.astype(jnp.bfloat16)
            else:
                queries[head, pl.ds(start, rows), :] = turned(part, qk_gain[0:1, :], start, rows)

    def begin_of(row):
        begin, bound = jnp.zeros_like(row), 0
        for index in range(8):
            bound = bound + lengths[0, index]
            begin = jnp.where(row >= bound, bound, begin)
        return begin

    def make_tables(block):
        row = block * BLOCK + lax.broadcasted_iota(jnp.int32, (BLOCK, 128), 0)
        angle = (row - begin_of(row)).astype(jnp.float32) * freq[...]
        lane = lax.broadcasted_iota(jnp.int32, (BLOCK, 128), 1)
        rows = slice(block * BLOCK, (block + 1) * BLOCK)
        cosine[rows, :] = jnp.cos(angle)
        sine[rows, :] = jnp.where(lane < 64, -1.0, 1.0) * jnp.sin(angle)

    def make_bias(block):
        low = max(block - 2, 0) * BLOCK
        row = block * BLOCK + lax.broadcasted_iota(jnp.int32, (BLOCK, 1), 0)
        column = low + lax.broadcasted_iota(jnp.int32, (BLOCK, WINDOW), 1)
        bias[block] = jnp.where((column >= begin_of(row)) & (column <= row), 0.0, -1e30)

    def attend(block, first_head, heads):
        start = pl.multiple_of(block * BLOCK, BLOCK)
        low = pl.multiple_of(jnp.maximum(block - 2, 0) * BLOCK, BLOCK)

        def two_heads(index, carry):
            head = first_head + 2 * index
            pair_of = queries[pl.ds(head, 2), pl.ds(start, BLOCK), :].reshape(2 * BLOCK, 128)
            scores = lax.dot_general(
                pair_of,
                keys[pl.ds(low, WINDOW), :],
                (((1,), (1,)), ((), ())),
                preferred_element_type=jnp.float32,
            ).reshape(2, BLOCK, WINDOW)
            scores = scores * (128 ** (-0.5) * LOG2_E) + bias[block][None]
            raised = jnp.exp2(scores - jnp.max(scores, axis=-1, keepdims=True))
            total = jnp.sum(raised, axis=-1, keepdims=True)
            mixed = jnp.dot(
                raised.astype(jnp.bfloat16).reshape(2 * BLOCK, WINDOW),
                values[pl.ds(low, WINDOW), :],
                preferred_element_type=jnp.float32,
            ).reshape(2, BLOCK, 128)
            mixed = (mixed / total).astype(jnp.bfloat16)
            for side in range(2):
                lanes = pl.ds(pl.multiple_of((head + side) * 128, 128), 128)
                context[pl.ds(start, BLOCK), lanes] = mixed[side]
            return carry

        lax.fori_loop(0, heads // 2, two_heads, 0)

    own_mine, own_other = normed.at[0:BLOCK, :], normed.at[BLOCK : 2 * BLOCK, :]

    def chunk_columns(index):
        order = ((0, 0), (0, 1), (1, 0), (1, 1), (3, 0), (3, 1), (2, 0), (2, 1))
        step, half = order[index]
        place = wrap(x + step) * 2 + lax.rem(y // 2 + half, 2)
        return pl.multiple_of(place * CHUNK, 128)

    def column_of(ref, index):
        return ref.at[:, pl.ds(chunk_columns(index), CHUNK)]

    def out_part(block, target, index):
        start = pl.multiple_of(block * BLOCK, BLOCK)
        part = lax.dot_general(
            context[pl.ds(start, BLOCK), :],
            wo[pl.ds(chunk_columns(index), CHUNK), :],
            (((1,), (1,)), ((), ())),
            preferred_element_type=jnp.float32,
        )
        column_of(target, index)[...] = part.astype(jnp.bfloat16)

    def far_half(block, side):
        return far_parts.at[pl.ds(pl.multiple_of(block * BLOCK + side * 128, 128), 128), :]

    def sib_half(block):
        return sib_far.at[block * 128 : (block + 1) * 128, :]

    def out_far(index, block):
        out_part(far * 2 + block, far_parts.at[block * BLOCK : (block + 1) * BLOCK, :], index)
        send(
            column_of(far_half(block, 1 - core), index),
            column_of(sib_half(block), index),
            out_send.at[index * 2 + block],
            out_recv.at[index * 2 + block],
            sibling,
        )

    def sum_half(side):
        return far_sum.at[pl.ds(pl.multiple_of(side * 128, 128), 128), :]

    def out_far_sum(index, block):
        await_recv(column_of(sib_half(block), index), out_recv.at[index * 2 + block])
        piece = column_of(far_half(block, core), index)
        piece[...] = (
            piece[...].astype(jnp.float32)
            + column_of(sib_half(block), index)[...].astype(jnp.float32)
        ).astype(jnp.bfloat16)
        send(
            piece,
            column_of(sum_half(core), index),
            out_send.at[16 + index * 2 + block],
            out_recv.at[16 + index * 2 + core],
            (dp, far * 2 + block),
        )

    def out_own(index):
        out_part(near * 2 + 1 - core, own_other, index)
        out_part(near * 2 + core, own_mine, index)
        send(
            column_of(own_other, index),
            column_of(sib_own, index),
            out_send.at[32 + index],
            out_recv.at[32 + index],
            sibling,
        )

    def out_final(index):
        await_recv(column_of(sib_own, index), out_recv.at[32 + index])
        for side in range(2):
            await_recv(column_of(sum_half(side), index), out_recv.at[16 + index * 2 + side])
        total = column_of(own_mine, index)[...].astype(jnp.float32)
        total = total + column_of(sib_own, index)[...].astype(jnp.float32)
        total = total + column_of(far_sum, index)[...].astype(jnp.float32)
        total = total + column_of(rows_in, index)[...].astype(jnp.float32)
        column_of(rows_in, index)[...] = total.astype(jnp.bfloat16)
        copy = pltpu.make_async_copy(
            column_of(rows_in, index), column_of(scored, index), store_sem.at[index]
        )
        copy.start()
        stores.append(copy)

    def both(step, unit, *rest):
        for half in range(2):
            step(unit, half, *rest)

    along_x, along_y = half_of(0), half_of(1)
    mate, other = 1 + 2 * lax.rem(y, 2), 3 - 2 * lax.rem(y, 2)

    pair_start(0)
    ring_open(0, 0)
    load_rows.wait()
    for step in range(NORM_STEPS):
        norm_step(step)
    ring_open(0, 1)
    pair_start(1)
    pair_start(2)
    for step in range(NORM_STEPS):
        norm_beside(step)
    norm_across(0)
    both(ring_first, 0, 1)
    both(ring_first, 0, 3)
    norm_across(1)
    both(ring_first, 0, 2)
    both(ring_open, 1)
    both(ring_second, 0, 0)
    both(ring_first, 1, 1)
    pair_start(OUT)
    norm_across(2)
    make_tables(0)
    make_bias(0)
    both(ring_second, 0, 1)
    both(ring_first, 1, 3)
    make_tables(1)
    make_bias(1)
    both(ring_second, 0, 3)
    both(ring_first, 1, 2)
    norm_across(3)
    make_tables(2)
    make_bias(2)
    both(ring_second, 0, 2)
    both(ring_open, 2)
    make_tables(3)
    make_bias(3)
    norm_forward(0)
    for a in range(4):
        both(ring_last, 0, a)
    both(ring_second, 1, 0)
    both(ring_first, 2, 1)
    project(0, near, 0, 256)
    both(ring_second, 1, 1)
    both(ring_first, 2, 3)
    project(0, near, 256, 256)
    both(ring_second, 1, 3)
    both(ring_first, 2, 2)
    norm_forward(1)
    both(ring_second, 1, 2)
    norm_far(0)
    norm_far(1)
    project(0, far, 0, 256)
    for a in range(4):
        both(ring_last, 1, a)
    both(ring_second, 2, 0)
    project(1, near, 0, 256)
    both(ring_second, 2, 1)
    both(ring_second, 2, 3)
    both(ring_second, 2, 2)
    ring_open(OUT, 0)
    project(1, near, 256, 256)
    project(1, far, 0, 256)
    ring_open(OUT, 1)
    norm_forward(2)
    attend(far * 2, 0, 4)
    for a in range(4):
        both(ring_last, 2, a)
    project(2, far, 0, 256)
    attend(far * 2, 4, 2)
    ring_head(OUT, 0, 1)
    ring_head(OUT, 0, 3)
    ring_second(OUT, 0, 0)
    norm_forward(3)
    attend(far * 2, 6, 2)
    norm_far(2)
    norm_far(3)
    project(0, far, 256, 256)
    ring_head(OUT, 1, 1)
    ring_head(OUT, 1, 3)
    ring_second(OUT, 1, 0)
    out_far(0, 0)
    spread(OUT, along_x, 1)
    spread(OUT, along_y, mate)
    project(1, far, 256, 256)
    out_far_sum(0, 0)
    project(2, far, 256, 256)
    ring_head(OUT, 0, 2)
    spread(OUT, along_x, 3)
    spread(OUT, along_y, other)
    attend(far * 2 + 1, 0, 4)
    ring_head(OUT, 1, 2)
    attend(far * 2 + 1, 4, 4)
    out_far(0, 1)
    spread(OUT, along_y, 2)
    turn_last(OUT, 0, 0)
    out_far(1, 0)
    out_far_sum(0, 1)
    out_far(1, 1)
    out_far_sum(1, 0)
    project(2, near, 0, 256)
    out_far_sum(1, 1)
    project(2, near, 256, 256)
    ring_second(OUT, along_x, 1)
    ring_second(OUT, along_y, mate, False)
    spread(OUT, along_x, 2)
    out_far(2, 0)
    out_far(2, 1)
    ring_second(OUT, along_x, 3)
    out_far_sum(2, 0)
    out_far_sum(2, 1)
    out_far(4, 0)
    out_far(4, 1)
    ring_second(OUT, along_y, other, True)
    out_far_sum(4, 0)
    out_far_sum(4, 1)
    attend(near * 2, 0, 8)
    turn_last(OUT, 0, 1)
    ring_second(OUT, along_y, 2)
    turn_last(OUT, 0, 3)
    ring_second(OUT, along_x, 2)
    for block in range(2):
        out_far(3, block)
    for block in range(2):
        out_far(5, block)
        out_far_sum(3, block)
    for block in range(2):
        out_far_sum(5, block)
    attend(near * 2 + 1, 0, 8)
    for copy in norm_copies:
        copy.wait_send()
    for index in range(2):
        out_own(index)
    turn_last(OUT, 0, 2)
    for a in range(4):
        turn_last(OUT, 1, a)
    for block in range(2):
        out_far(6, block)
    for block in range(2):
        out_far(7, block)
        out_far_sum(6, block)
    for block in range(2):
        out_far_sum(7, block)
    for index in range(2, STEPS):
        out_own(index)
    for index in range(STEPS):
        out_final(index)
    for copy in sends:
        copy.wait_send()
    for copy in stores:
        copy.wait()


def layer(weights, o_weight, states, norm_gain, qk_gain, lengths, freq):
    bf16, f32 = jnp.bfloat16, jnp.float32
    width = states.shape[1]
    tokens = 4 * BLOCK
    vmem = pl.BlockSpec(memory_space=pltpu.VMEM)
    hbm = pl.BlockSpec(memory_space=pl.ANY)
    return pl.pallas_call(
        layer_kernel,
        out_shape=jax.ShapeDtypeStruct(states.shape, bf16),
        in_specs=[hbm, hbm, hbm, vmem, vmem, pl.BlockSpec(memory_space=pltpu.SMEM), vmem],
        out_specs=hbm,
        scratch_shapes=[
            *[pltpu.VMEM((width, columns), bf16) for columns in WIDTHS],
            pltpu.VMEM((tokens, width), bf16),
            pltpu.VMEM((BLOCK, width), bf16),
            pltpu.VMEM((8, tokens, 128), bf16),
            pltpu.VMEM((tokens, 128), bf16),
            pltpu.VMEM((tokens, 128), bf16),
            pltpu.VMEM((tokens, 1024), bf16),
            pltpu.VMEM((4, BLOCK, WINDOW), f32),
            pltpu.VMEM((tokens, 128), f32),
            pltpu.VMEM((tokens, 128), f32),
            pltpu.VMEM((2 * BLOCK, width), bf16),
            *[pltpu.VMEM((BLOCK, width), bf16) for _ in range(3)],
            pltpu.SemaphoreType.DMA((5,)),
            pltpu.SemaphoreType.DMA((128,)),
            pltpu.SemaphoreType.DMA((128,)),
            pltpu.SemaphoreType.DMA((4,)),
            pltpu.SemaphoreType.DMA((4,)),
            pltpu.SemaphoreType.DMA((12,)),
            pltpu.SemaphoreType.DMA((12,)),
            pltpu.SemaphoreType.DMA((40,)),
            pltpu.SemaphoreType.DMA((40,)),
            pltpu.SemaphoreType.DMA((STEPS,)),
        ],
        compiler_params=pltpu.CompilerParams(
            collective_id=1, has_side_effects=True, vmem_limit_bytes=62 * 2**20
        ),
        cost_estimate=pl.CostEstimate(
            flops=30_000_000_000, bytes_accessed=10_000_000, transcendentals=5_000_000
        ),
        name="layer",
    )(weights, o_weight, states, norm_gain, qk_gain, lengths, freq)


def per_device(
    states,
    lengths,
    norm_gain,
    qk_gain,
    q_master,
    q_grad,
    q_moments,
    kv_master,
    kv_grad,
    kv_moments,
    o_master,
    o_grad,
    o_moments,
):
    q_new, q_moments_new, kv_new, kv_moments_new, o_new, o_moments_new, weights, o_weight = adam(
        q_master,
        q_grad,
        q_moments,
        kv_master,
        kv_grad,
        kv_moments,
        o_master,
        o_grad,
        o_moments,
    )
    head = qk_gain.shape[1]
    half = np.arange(head // 2) * 2.0 / head
    freq = np.tile(rope_base**-half, 2)[None, :].astype(np.float32)
    scored = layer(
        weights, o_weight, states, norm_gain[None, :], qk_gain, lengths, jnp.asarray(freq)
    )
    return (scored, q_new, q_moments_new, kv_new, kv_moments_new, o_new, o_moments_new)


def solution(mesh):
    return jax.shard_map(
        per_device,
        mesh=mesh,
        in_specs=(
            P(("dp", "tensor"), None),
            P("dp", None),
            P(),
            P(),
            P("dp", "tensor"),
            P("dp", "tensor"),
            P(None, "dp", "tensor"),
            P(None, "dp", "tensor"),
            P(None, "dp", "tensor"),
            P(None, None, "dp", "tensor"),
            P("dp", "tensor"),
            P("dp", "tensor"),
            P(None, "dp", "tensor"),
        ),
        out_specs=(
            P(("dp", "tensor"), None),
            P("dp", "tensor"),
            P(None, "dp", "tensor"),
            P(None, "dp", "tensor"),
            P(None, None, "dp", "tensor"),
            P("dp", "tensor"),
            P(None, "dp", "tensor"),
        ),
        check_vma=False,
    )
```

```python
import jax
import jax.numpy as jnp
import numpy as np
from jax import lax
from jax.experimental import pallas as pl
from jax.experimental.pallas import tpu as pltpu
from jax.sharding import PartitionSpec as P

beta_one = 0.9
beta_two = 0.95
adam_eps = 1e-08
learn_rate = 0.001
decay_rate = 0.1
step_count = 100.0
norm_eps = 1e-06
rope_base = 1000000.0
LOG2_E = 1.4426950408889634

MESH = pl.DeviceIdType.MESH
ROWS = 160
SIDE = 4
BLOCK = 256
CHUNK = 640
STEPS = 8
WIDTHS = (512, 512, 256, 1024)
STARTS = (0, 512, 1024)
OUT = 3
NORM_ROWS = 64
NORM_STEPS = BLOCK // NORM_ROWS
WINDOW = 768


def adam_update(master, grad, first, second):
    grad_full = grad.astype(jnp.float32)
    first = beta_one * first + (1.0 - beta_one) * grad_full
    second = beta_two * second + (1.0 - beta_two) * grad_full * grad_full
    ratio = (
        first
        / (1.0 - beta_one**step_count)
        / (jnp.sqrt(second / (1.0 - beta_two**step_count)) + adam_eps)
    )
    return (master - learn_rate * (ratio + decay_rate * master), first, second)


def adam_kernel(
    q_master,
    q_grad,
    q_moments,
    kv_master,
    kv_grad,
    kv_moments,
    o_master,
    o_grad,
    o_moments,
    q_new,
    q_moments_new,
    kv_new,
    kv_moments_new,
    o_new,
    o_moments_new,
    weights,
    o_weight,
):
    for master, grad, moments, new, moments_new, low in (
        (q_master, q_grad, q_moments, q_new, q_moments_new, weights.at[:, 256:]),
        (o_master, o_grad, o_moments, o_new, o_moments_new, o_weight),
    ):
        updated, first, second = adam_update(master[...], grad[...], moments[0], moments[1])
        new[...] = updated
        moments_new[0] = first
        moments_new[1] = second
        low[...] = updated.astype(jnp.bfloat16)
    for index in range(2):
        updated, first, second = adam_update(
            kv_master[index], kv_grad[index], kv_moments[0, index], kv_moments[1, index]
        )
        kv_new[index] = updated
        kv_moments_new[0, index] = first
        kv_moments_new[1, index] = second
        weights[:, index * 128 : (index + 1) * 128] = updated.astype(jnp.bfloat16)


def adam(*arrays):
    rows = 80
    steps = ROWS // rows

    def spec(shape):
        lead = len(shape) - 2
        return pl.BlockSpec(
            shape[:lead] + (rows, shape[-1]), lambda step: (0,) * lead + (step, 0)
        )

    shapes = [array.shape for array in arrays]
    made = [(shapes[index], jnp.float32) for index in (0, 2, 3, 5, 6, 8)]
    made = made + [((ROWS, 1280), jnp.bfloat16), ((ROWS, 1024), jnp.bfloat16)]
    return pl.pallas_call(
        adam_kernel,
        grid=(steps,),
        out_shape=[jax.ShapeDtypeStruct(shape, kind) for shape, kind in made],
        in_specs=[spec(shape) for shape in shapes],
        out_specs=[spec(shape) for shape, _ in made],
        compiler_params=pltpu.CompilerParams(vmem_limit_bytes=62 * 2**20),
        name="adam",
    )(*arrays)


def layer_kernel(
    weights,
    o_weight,
    states,
    norm_gain,
    qk_gain,
    lengths,
    freq,
    scored,
    w0,
    w1,
    w2,
    wo,
    normed,
    rows_in,
    queries,
    keys,
    values,
    context,
    bias,
    cosine,
    sine,
    far_parts,
    sib_far,
    sib_own,
    far_sum,
    local_sem,
    ring_send,
    ring_recv,
    pair_send,
    pair_recv,
    norm_send,
    norm_recv,
    out_send,
    out_recv,
    store_sem,
):
    dp = lax.axis_index("dp")
    tensor = lax.axis_index("tensor")
    x, y, z_lo = dp // 8, (dp // 2) % 4, dp % 2
    z_hi, core = tensor // 2, tensor % 2
    near, far = z_hi, 1 - z_hi
    units = (w0, w1, w2, wo)

    sibling = (dp, z_hi * 2 + 1 - core)
    across = (dp, (1 - z_hi) * 2 + core)
    pair = (dp + 1 - 2 * z_lo, tensor)

    def wrap(value):
        return lax.rem(value + SIDE, SIDE)

    def plane(px, py):
        return (wrap(px) * 8 + wrap(py) * 2 + z_lo, tensor)

    barrier = pltpu.get_barrier_semaphore()
    partners = (
        plane(x + 1, y),
        plane(x - 1, y),
        plane(x, y + 1),
        plane(x, y - 1),
        pair,
        across,
        (dp, (1 - z_hi) * 2 + 1 - core),
        sibling,
    )
    for partner in partners:
        pl.semaphore_signal(barrier, inc=1, device_id=partner, device_id_type=MESH)

    def shard(unit, source):
        return units[unit].at[pl.ds(pl.multiple_of(source * ROWS, 32), ROWS), :]

    loads = []
    for unit in range(3):
        loads.append(
            pltpu.make_async_copy(
                weights.at[:, pl.ds(STARTS[unit], WIDTHS[unit])],
                shard(unit, dp),
                local_sem.at[unit],
            )
        )
    loads.append(pltpu.make_async_copy(o_weight, shard(OUT, dp), local_sem.at[OUT]))
    load_rows = pltpu.make_async_copy(states, rows_in, local_sem.at[4])
    loads[0].start()
    load_rows.start()
    for load in loads[1:]:
        load.start()

    pl.semaphore_wait(barrier, len(partners))

    sends = []
    norm_copies = []
    stores = []

    def send(src, dst, send_sem, recv_sem, device, sends=sends):
        copy = pltpu.make_async_remote_copy(
            src_ref=src,
            dst_ref=dst,
            send_sem=send_sem,
            recv_sem=recv_sem,
            device_id=device,
            device_id_type=MESH,
        )
        copy.start()
        sends.append(copy)
        return copy

    def await_recv(dst, recv_sem):
        pltpu.make_async_remote_copy(
            src_ref=dst,
            dst_ref=dst,
            send_sem=pair_send.at[0],
            recv_sem=recv_sem,
            device_id=sibling,
            device_id_type=MESH,
        ).wait_recv()

    def flavour(half):
        return z_lo + half * (1 - 2 * z_lo)

    def ring_pos(half):
        turn = flavour(half)
        return (x + turn * (y - x), y + turn * (x - y))

    def ring_place(half, first, second):
        turn = flavour(half)
        first, second = wrap(first), wrap(second)
        return (first + turn * (second - first), second + turn * (first - second))

    def ring_device(half, first, second):
        px, py = ring_place(half, first, second)
        return (px * 8 + py * 2 + z_lo, tensor)

    def ring_shard(unit, half, first, second):
        px, py = ring_place(half, first, second)
        return shard(unit, px * 8 + py * 2 + flavour(half))

    def ring_recv_sem(unit, half, a, b):
        return ring_recv.at[(unit * 2 + half) * 16 + a * 4 + b]

    def ring_send_sem(unit, half, index):
        return ring_send.at[(unit * 2 + half) * 16 + index]

    def pair_start(unit):
        loads[unit].wait()
        send(shard(unit, dp), shard(unit, dp), pair_send.at[unit], pair_recv.at[unit], pair)

    def spread(unit, half, a):
        first, second = ring_pos(half)
        piece = ring_shard(unit, half, first + a, second)
        for index, (step, b) in enumerate(((1, 3), (-1, 1))):
            send(
                piece,
                piece,
                ring_send_sem(unit, half, 3 + 2 * a + index),
                ring_recv_sem(unit, half, a, b),
                ring_device(half, first, second + step),
            )

    def ring_open(unit, half):
        first, second = ring_pos(half)
        piece = ring_shard(unit, half, first, second)
        if half == 1:
            await_recv(piece, pair_recv.at[unit])
        for index, (step, a) in enumerate(((1, 3), (-1, 1))):
            send(
                piece,
                piece,
                ring_send_sem(unit, half, index),
                ring_recv_sem(unit, half, a, 0),
                ring_device(half, first + step, second),
            )
        spread(unit, half, 0)

    def ring_head(unit, half, a):
        first, second = ring_pos(half)
        piece = ring_shard(unit, half, first + a, second)
        await_recv(piece, ring_recv_sem(unit, half, a, 0))
        upward = unit != OUT and (half + (unit in (1, 2))) % 2 == 0
        if a == (3 if upward else 1):
            step = 1 if upward else -1
            send(
                piece,
                piece,
                ring_send_sem(unit, half, 2),
                ring_recv_sem(unit, half, 2, 0),
                ring_device(half, first + step, second),
            )

    def ring_first(unit, half, a):
        ring_head(unit, half, a)
        spread(unit, half, a)

    def ring_second(unit, half, a, upward=None):
        first, second = ring_pos(half)
        upward = a in (0, 3) if upward is None else upward
        for b in (1, 3):
            piece = ring_shard(unit, half, first + a, second + b)
            await_recv(piece, ring_recv_sem(unit, half, a, b))
            if b == (3 if upward else 1):
                step = 1 if upward else -1
                send(
                    piece,
                    piece,
                    ring_send_sem(unit, half, 11 + a),
                    ring_recv_sem(unit, half, a, 2),
                    ring_device(half, first, second + step),
                )

    def ring_last(unit, half, a):
        first, second = ring_pos(half)
        piece = ring_shard(unit, half, first + a, second + 2)
        await_recv(piece, ring_recv_sem(unit, half, a, 2))

    def half_of(turn):
        return turn + z_lo * (1 - 2 * turn)

    def turn_last(unit, turn, a):
        half = half_of(turn)
        px, py = (wrap(x + a), wrap(y + 2)) if turn == 0 else (wrap(x + 2), wrap(y + a))
        await_recv(shard(unit, px * 8 + py * 2 + turn), ring_recv_sem(unit, half, a, 2))

    def norm_rows(block, step):
        start = pl.multiple_of(block * BLOCK + step * NORM_ROWS, NORM_ROWS)
        return normed.at[pl.ds(start, NORM_ROWS), :]

    def norm_step(step):
        full = rows_in[step * NORM_ROWS : (step + 1) * NORM_ROWS, :].astype(jnp.float32)
        scale = lax.rsqrt(jnp.mean(full * full, axis=-1, keepdims=True) + norm_eps)
        piece = norm_rows(tensor, step)
        piece[...] = (full * scale * norm_gain[...]).astype(jnp.bfloat16)
        send(piece, piece, norm_send.at[4 + step], norm_recv.at[4 + step], sibling, norm_copies)

    def norm_beside(step):
        await_recv(norm_rows(z_hi * 2 + 1 - core, step), norm_recv.at[4 + step])

    def half_rows(chip, step, side):
        start = pl.multiple_of(chip * 512 + step * 128 + side * 64, 64)
        return normed.at[pl.ds(start, 64), :]

    def norm_across(step):
        piece = half_rows(near, step, core)
        send(piece, piece, norm_send.at[step], norm_recv.at[step], across, norm_copies)

    def norm_forward(step):
        piece = half_rows(far, step, core)
        await_recv(piece, norm_recv.at[step])
        send(piece, piece, norm_send.at[8 + step], norm_recv.at[8 + step], sibling, norm_copies)

    def norm_far(step):
        await_recv(half_rows(far, step, 1 - core), norm_recv.at[8 + step])

    def turned(raw, gain, start, rows):
        scale = lax.rsqrt(jnp.mean(raw * raw, axis=-1, keepdims=True) + norm_eps)
        flat = raw * scale * gain
        return (
            flat * cosine[pl.ds(start, rows), :]
            + pltpu.roll(flat, 64, 1) * sine[pl.ds(start, rows), :]
        ).astype(jnp.bfloat16)

    def project(unit, chip, offset, rows):
        start = pl.multiple_of(chip * 512 + offset, 128)
        raw = jnp.dot(
            normed[pl.ds(start, rows), :], units[unit][...], preferred_element_type=jnp.float32
        )
        for column in range(WIDTHS[unit] // 128):
            part = raw[:, column * 128 : (column + 1) * 128]
            head = STARTS[unit] // 128 + column - 2
            if head == -2:
                keys[pl.ds(start, rows), :] = turned(part, qk_gain[1:2, :], start, rows)
            elif head == -1:
                values[pl.ds(start, rows), :] = part.astype(jnp.bfloat16)
            else:
                queries[head, pl.ds(start, rows), :] = turned(part, qk_gain[0:1, :], start, rows)

    def begin_of(row):
        begin, bound = jnp.zeros_like(row), 0
        for index in range(8):
            bound = bound + lengths[0, index]
            begin = jnp.where(row >= bound, bound, begin)
        return begin

    def make_tables(block):
        row = block * BLOCK + lax.broadcasted_iota(jnp.int32, (BLOCK, 128), 0)
        angle = (row - begin_of(row)).astype(jnp.float32) * freq[...]
        lane = lax.broadcasted_iota(jnp.int32, (BLOCK, 128), 1)
        rows = slice(block * BLOCK, (block + 1) * BLOCK)
        cosine[rows, :] = jnp.cos(angle)
        sine[rows, :] = jnp.where(lane < 64, -1.0, 1.0) * jnp.sin(angle)

    def make_bias(block):
        low = max(block - 2, 0) * BLOCK
        row = block * BLOCK + lax.broadcasted_iota(jnp.int32, (BLOCK, 1), 0)
        column = low + lax.broadcasted_iota(jnp.int32, (BLOCK, WINDOW), 1)
        bias[block] = jnp.where((column >= begin_of(row)) & (column <= row), 0.0, -1e30)

    def attend(block, first_head, heads):
        start = pl.multiple_of(block * BLOCK, BLOCK)
        low = pl.multiple_of(jnp.maximum(block - 2, 0) * BLOCK, BLOCK)

        def two_heads(index, carry):
            head = first_head + 2 * index
            pair_of = queries[pl.ds(head, 2), pl.ds(start, BLOCK), :].reshape(2 * BLOCK, 128)
            scores = lax.dot_general(
                pair_of,
                keys[pl.ds(low, WINDOW), :],
                (((1,), (1,)), ((), ())),
                preferred_element_type=jnp.float32,
            ).reshape(2, BLOCK, WINDOW)
            scores = scores * (128 ** (-0.5) * LOG2_E) + bias[block][None]
            raised = jnp.exp2(scores - jnp.max(scores, axis=-1, keepdims=True))
            total = jnp.sum(raised, axis=-1, keepdims=True)
            mixed = jnp.dot(
                raised.astype(jnp.bfloat16).reshape(2 * BLOCK, WINDOW),
                values[pl.ds(low, WINDOW), :],
                preferred_element_type=jnp.float32,
            ).reshape(2, BLOCK, 128)
            mixed = (mixed / total).astype(jnp.bfloat16)
            for side in range(2):
                lanes = pl.ds(pl.multiple_of((head + side) * 128, 128), 128)
                context[pl.ds(start, BLOCK), lanes] = mixed[side]
            return carry

        lax.fori_loop(0, heads // 2, two_heads, 0, unroll=True)

    own_mine, own_other = normed.at[0:BLOCK, :], normed.at[BLOCK : 2 * BLOCK, :]

    def chunk_columns(index):
        order = ((0, 0), (0, 1), (1, 0), (1, 1), (3, 0), (3, 1), (2, 0), (2, 1))
        step, half = order[index]
        place = wrap(x + step) * 2 + lax.rem(y // 2 + half, 2)
        return pl.multiple_of(place * CHUNK, 128)

    def column_of(ref, index):
        return ref.at[:, pl.ds(chunk_columns(index), CHUNK)]

    def out_part(block, target, index):
        start = pl.multiple_of(block * BLOCK, BLOCK)
        part = lax.dot_general(
            context[pl.ds(start, BLOCK), :],
            wo[pl.ds(chunk_columns(index), CHUNK), :],
            (((1,), (1,)), ((), ())),
            preferred_element_type=jnp.float32,
        )
        column_of(target, index)[...] = part.astype(jnp.bfloat16)

    def far_half(block, side):
        return far_parts.at[pl.ds(pl.multiple_of(block * BLOCK + side * 128, 128), 128), :]

    def sib_half(block):
        return sib_far.at[block * 128 : (block + 1) * 128, :]

    def out_far(index, block):
        out_part(far * 2 + block, far_parts.at[block * BLOCK : (block + 1) * BLOCK, :], index)
        send(
            column_of(far_half(block, 1 - core), index),
            column_of(sib_half(block), index),
            out_send.at[index * 2 + block],
            out_recv.at[index * 2 + block],
            sibling,
        )

    def sum_half(side):
        return far_sum.at[pl.ds(pl.multiple_of(side * 128, 128), 128), :]

    def out_far_sum(index, block):
        await_recv(column_of(sib_half(block), index), out_recv.at[index * 2 + block])
        piece = column_of(far_half(block, core), index)
        piece[...] = (
            piece[...].astype(jnp.float32)
            + column_of(sib_half(block), index)[...].astype(jnp.float32)
        ).astype(jnp.bfloat16)
        send(
            piece,
            column_of(sum_half(core), index),
            out_send.at[16 + index * 2 + block],
            out_recv.at[16 + index * 2 + core],
            (dp, far * 2 + block),
        )

    def out_own(index):
        out_part(near * 2 + 1 - core, own_other, index)
        out_part(near * 2 + core, own_mine, index)
        send(
            column_of(own_other, index),
            column_of(sib_own, index),
            out_send.at[32 + index],
            out_recv.at[32 + index],
            sibling,
        )

    def out_final(index):
        await_recv(column_of(sib_own, index), out_recv.at[32 + index])
        for side in range(2):
            await_recv(column_of(sum_half(side), index), out_recv.at[16 + index * 2 + side])
        total = column_of(own_mine, index)[...].astype(jnp.float32)
        total = total + column_of(sib_own, index)[...].astype(jnp.float32)
        total = total + column_of(far_sum, index)[...].astype(jnp.float32)
        total = total + column_of(rows_in, index)[...].astype(jnp.float32)
        column_of(rows_in, index)[...] = total.astype(jnp.bfloat16)
        copy = pltpu.make_async_copy(
            column_of(rows_in, index), column_of(scored, index), store_sem.at[index]
        )
        copy.start()
        stores.append(copy)

    def both(step, unit, *rest):
        for half in range(2):
            step(unit, half, *rest)

    along_x, along_y = half_of(0), half_of(1)
    mate, other = 1 + 2 * lax.rem(y, 2), 3 - 2 * lax.rem(y, 2)

    pair_start(0)
    ring_open(0, 0)
    load_rows.wait()
    for step in range(NORM_STEPS):
        norm_step(step)
    ring_open(0, 1)
    pair_start(1)
    pair_start(2)
    for step in range(NORM_STEPS):
        norm_beside(step)
    norm_across(0)
    both(ring_first, 0, 1)
    both(ring_first, 0, 3)
    norm_across(1)
    both(ring_first, 0, 2)
    both(ring_open, 1)
    both(ring_second, 0, 0)
    both(ring_first, 1, 1)
    pair_start(OUT)
    norm_across(2)
    make_tables(0)
    make_bias(0)
    both(ring_second, 0, 1)
    both(ring_first, 1, 3)
    make_tables(1)
    make_bias(1)
    both(ring_second, 0, 3)
    both(ring_first, 1, 2)
    norm_across(3)
    make_tables(2)
    make_bias(2)
    both(ring_second, 0, 2)
    both(ring_open, 2)
    make_tables(3)
    make_bias(3)
    norm_forward(0)
    for a in range(4):
        both(ring_last, 0, a)
    both(ring_second, 1, 0)
    both(ring_first, 2, 1)
    project(0, near, 0, 256)
    both(ring_second, 1, 1)
    both(ring_first, 2, 3)
    project(0, near, 256, 256)
    both(ring_second, 1, 3)
    both(ring_first, 2, 2)
    norm_forward(1)
    both(ring_second, 1, 2)
    norm_far(0)
    norm_far(1)
    project(0, far, 0, 256)
    for a in range(4):
        both(ring_last, 1, a)
    both(ring_second, 2, 0)
    project(1, near, 0, 256)
    both(ring_second, 2, 1)
    both(ring_second, 2, 3)
    both(ring_second, 2, 2)
    ring_open(OUT, 0)
    project(1, near, 256, 256)
    project(1, far, 0, 256)
    ring_open(OUT, 1)
    norm_forward(2)
    attend(far * 2, 0, 4)
    for a in range(4):
        both(ring_last, 2, a)
    project(2, far, 0, 256)
    attend(far * 2, 4, 2)
    ring_head(OUT, 0, 1)
    ring_head(OUT, 0, 3)
    ring_second(OUT, 0, 0)
    norm_forward(3)
    attend(far * 2, 6, 2)
    norm_far(2)
    norm_far(3)
    project(0, far, 256, 256)
    ring_head(OUT, 1, 1)
    ring_head(OUT, 1, 3)
    ring_second(OUT, 1, 0)
    out_far(0, 0)
    spread(OUT, along_x, 1)
    spread(OUT, along_y, mate)
    project(1, far, 256, 256)
    out_far_sum(0, 0)
    project(2, far, 256, 256)
    ring_head(OUT, 0, 2)
    spread(OUT, along_x, 3)
    spread(OUT, along_y, other)
    attend(far * 2 + 1, 0, 4)
    ring_head(OUT, 1, 2)
    turn_last(OUT, 0, 0)
    out_far(1, 0)
    spread(OUT, along_y, 2)
    out_far_sum(1, 0)
    attend(far * 2 + 1, 4, 4)
    out_far(0, 1)
    out_far(1, 1)
    out_far_sum(0, 1)
    project(2, near, 0, 256)
    out_far_sum(1, 1)
    project(2, near, 256, 256)
    ring_second(OUT, along_x, 1)
    ring_second(OUT, along_y, mate, False)
    out_far(2, 0)
    out_far(2, 1)
    out_far_sum(2, 0)
    out_far_sum(2, 1)
    ring_second(OUT, along_x, 3)
    spread(OUT, along_x, 2)
    out_far(4, 0)
    out_far(4, 1)
    ring_second(OUT, along_y, other, True)
    out_far_sum(4, 0)
    out_far_sum(4, 1)
    attend(near * 2, 0, 8)
    turn_last(OUT, 0, 1)
    ring_second(OUT, along_y, 2)
    for block in range(2):
        out_far(3, block)
    turn_last(OUT, 0, 3)
    for block in range(2):
        out_far(5, block)
        out_far_sum(3, block)
    for block in range(2):
        out_far_sum(5, block)
    attend(near * 2 + 1, 0, 8)
    ring_second(OUT, along_x, 2, True)
    for copy in norm_copies:
        copy.wait_send()
    for index in range(2):
        out_own(index)
    turn_last(OUT, 0, 2)
    for a in range(4):
        turn_last(OUT, 1, a)
    for block in range(2):
        out_far(6, block)
    for block in range(2):
        out_far(7, block)
        out_far_sum(6, block)
    for block in range(2):
        out_far_sum(7, block)
    for index in range(2, STEPS):
        out_own(index)
    for index in range(STEPS):
        out_final(index)
    for copy in sends:
        copy.wait_send()
    for copy in stores:
        copy.wait()


def layer(weights, o_weight, states, norm_gain, qk_gain, lengths, freq):
    bf16, f32 = jnp.bfloat16, jnp.float32
    width = states.shape[1]
    tokens = 4 * BLOCK
    vmem = pl.BlockSpec(memory_space=pltpu.VMEM)
    hbm = pl.BlockSpec(memory_space=pl.ANY)
    return pl.pallas_call(
        layer_kernel,
        out_shape=jax.ShapeDtypeStruct(states.shape, bf16),
        in_specs=[hbm, hbm, hbm, vmem, vmem, pl.BlockSpec(memory_space=pltpu.SMEM), vmem],
        out_specs=hbm,
        scratch_shapes=[
            *[pltpu.VMEM((width, columns), bf16) for columns in WIDTHS],
            pltpu.VMEM((tokens, width), bf16),
            pltpu.VMEM((BLOCK, width), bf16),
            pltpu.VMEM((8, tokens, 128), bf16),
            pltpu.VMEM((tokens, 128), bf16),
            pltpu.VMEM((tokens, 128), bf16),
            pltpu.VMEM((tokens, 1024), bf16),
            pltpu.VMEM((4, BLOCK, WINDOW), f32),
            pltpu.VMEM((tokens, 128), f32),
            pltpu.VMEM((tokens, 128), f32),
            pltpu.VMEM((2 * BLOCK, width), bf16),
            *[pltpu.VMEM((BLOCK, width), bf16) for _ in range(3)],
            pltpu.SemaphoreType.DMA((5,)),
            pltpu.SemaphoreType.DMA((128,)),
            pltpu.SemaphoreType.DMA((128,)),
            pltpu.SemaphoreType.DMA((4,)),
            pltpu.SemaphoreType.DMA((4,)),
            pltpu.SemaphoreType.DMA((12,)),
            pltpu.SemaphoreType.DMA((12,)),
            pltpu.SemaphoreType.DMA((40,)),
            pltpu.SemaphoreType.DMA((40,)),
            pltpu.SemaphoreType.DMA((STEPS,)),
        ],
        compiler_params=pltpu.CompilerParams(
            collective_id=1, has_side_effects=True, vmem_limit_bytes=62 * 2**20
        ),
        cost_estimate=pl.CostEstimate(
            flops=30_000_000_000, bytes_accessed=10_000_000, transcendentals=5_000_000
        ),
        name="layer",
    )(weights, o_weight, states, norm_gain, qk_gain, lengths, freq)


def per_device(
    states,
    lengths,
    norm_gain,
    qk_gain,
    q_master,
    q_grad,
    q_moments,
    kv_master,
    kv_grad,
    kv_moments,
    o_master,
    o_grad,
    o_moments,
):
    q_new, q_moments_new, kv_new, kv_moments_new, o_new, o_moments_new, weights, o_weight = adam(
        q_master,
        q_grad,
        q_moments,
        kv_master,
        kv_grad,
        kv_moments,
        o_master,
        o_grad,
        o_moments,
    )
    head = qk_gain.shape[1]
    half = np.arange(head // 2) * 2.0 / head
    freq = np.tile(rope_base**-half, 2)[None, :].astype(np.float32)
    scored = layer(
        weights, o_weight, states, norm_gain[None, :], qk_gain, lengths, jnp.asarray(freq)
    )
    return (scored, q_new, q_moments_new, kv_new, kv_moments_new, o_new, o_moments_new)


def solution(mesh):
    return jax.shard_map(
        per_device,
        mesh=mesh,
        in_specs=(
            P(("dp", "tensor"), None),
            P("dp", None),
            P(),
            P(),
            P("dp", "tensor"),
            P("dp", "tensor"),
            P(None, "dp", "tensor"),
            P(None, "dp", "tensor"),
            P(None, "dp", "tensor"),
            P(None, None, "dp", "tensor"),
            P("dp", "tensor"),
            P("dp", "tensor"),
            P(None, "dp", "tensor"),
        ),
        out_specs=(
            P(("dp", "tensor"), None),
            P("dp", "tensor"),
            P(None, "dp", "tensor"),
            P(None, "dp", "tensor"),
            P(None, None, "dp", "tensor"),
            P("dp", "tensor"),
            P(None, "dp", "tensor"),
        ),
        check_vma=False,
    )
```

```python
import jax
import jax.numpy as jnp
import numpy as np
from jax import lax
from jax.experimental import pallas as pl
from jax.experimental.pallas import tpu as pltpu
from jax.sharding import PartitionSpec as P

beta_one = 0.9
beta_two = 0.95
adam_eps = 1e-08
learn_rate = 0.001
decay_rate = 0.1
step_count = 100.0
first_scale = 1.0 / (1.0 - beta_one**step_count)
second_scale = 1.0 / (1.0 - beta_two**step_count)
norm_eps = 1e-06
rope_base = 1000000.0
LOG2_E = 1.4426950408889634

MESH = pl.DeviceIdType.MESH
ROWS = 160
SIDE = 4
BLOCK = 256
CHUNK = 640
STEPS = 8
WIDTHS = (512, 512, 256, 1024)
STARTS = (0, 512, 1024)
OUT = 3
NORM_ROWS = 64
NORM_STEPS = BLOCK // NORM_ROWS
WINDOW = 768


def adam_update(master, grad, first, second):
    grad_full = grad.astype(jnp.float32)
    first = beta_one * first + (1.0 - beta_one) * grad_full
    second = beta_two * second + (1.0 - beta_two) * grad_full * grad_full
    ratio = (first * first_scale) / (jnp.sqrt(second * second_scale) + adam_eps)
    return (master - learn_rate * (ratio + decay_rate * master), first, second)


def adam_kernel(
    q_master,
    q_grad,
    q_moments,
    kv_master,
    kv_grad,
    kv_moments,
    o_master,
    o_grad,
    o_moments,
    q_new,
    q_moments_new,
    kv_new,
    kv_moments_new,
    o_new,
    o_moments_new,
    weights,
    o_weight,
):
    for master, grad, moments, new, moments_new, low in (
        (q_master, q_grad, q_moments, q_new, q_moments_new, weights.at[:, 256:]),
        (o_master, o_grad, o_moments, o_new, o_moments_new, o_weight),
    ):
        updated, first, second = adam_update(master[...], grad[...], moments[0], moments[1])
        new[...] = updated
        moments_new[0] = first
        moments_new[1] = second
        low[...] = updated.astype(jnp.bfloat16)
    for index in range(2):
        updated, first, second = adam_update(
            kv_master[index], kv_grad[index], kv_moments[0, index], kv_moments[1, index]
        )
        kv_new[index] = updated
        kv_moments_new[0, index] = first
        kv_moments_new[1, index] = second
        weights[:, index * 128 : (index + 1) * 128] = updated.astype(jnp.bfloat16)


def adam(*arrays):
    rows = 80
    steps = ROWS // rows

    def spec(shape):
        lead = len(shape) - 2
        return pl.BlockSpec(
            shape[:lead] + (rows, shape[-1]), lambda step: (0,) * lead + (step, 0)
        )

    shapes = [array.shape for array in arrays]
    made = [(shapes[index], jnp.float32) for index in (0, 2, 3, 5, 6, 8)]
    made = made + [((ROWS, 1280), jnp.bfloat16), ((ROWS, 1024), jnp.bfloat16)]
    return pl.pallas_call(
        adam_kernel,
        grid=(steps,),
        out_shape=[jax.ShapeDtypeStruct(shape, kind) for shape, kind in made],
        in_specs=[spec(shape) for shape in shapes],
        out_specs=[spec(shape) for shape, _ in made],
        compiler_params=pltpu.CompilerParams(vmem_limit_bytes=62 * 2**20),
        name="adam",
    )(*arrays)


def layer_kernel(
    weights,
    o_weight,
    states,
    norm_gain,
    qk_gain,
    lengths,
    freq,
    scored,
    w0,
    w1,
    w2,
    wo,
    normed,
    rows_in,
    queries,
    keys,
    values,
    context,
    bias,
    cosine,
    sine,
    far_parts,
    sib_far,
    sib_own,
    far_sum,
    local_sem,
    ring_send,
    ring_recv,
    pair_send,
    pair_recv,
    norm_send,
    norm_recv,
    out_send,
    out_recv,
    store_sem,
):
    dp = lax.axis_index("dp")
    tensor = lax.axis_index("tensor")
    x, y, z_lo = dp // 8, (dp // 2) % 4, dp % 2
    z_hi, core = tensor // 2, tensor % 2
    near, far = z_hi, 1 - z_hi
    units = (w0, w1, w2, wo)

    sibling = (dp, z_hi * 2 + 1 - core)
    across = (dp, (1 - z_hi) * 2 + core)
    pair = (dp + 1 - 2 * z_lo, tensor)

    def wrap(value):
        return lax.rem(value + SIDE, SIDE)

    def plane(px, py):
        return (wrap(px) * 8 + wrap(py) * 2 + z_lo, tensor)

    barrier = pltpu.get_barrier_semaphore()
    partners = (
        plane(x + 1, y),
        plane(x - 1, y),
        plane(x, y + 1),
        plane(x, y - 1),
        pair,
        across,
        (dp, (1 - z_hi) * 2 + 1 - core),
        sibling,
    )
    for partner in partners:
        pl.semaphore_signal(barrier, inc=1, device_id=partner, device_id_type=MESH)

    def shard(unit, source):
        return units[unit].at[pl.ds(pl.multiple_of(source * ROWS, 32), ROWS), :]

    loads = []
    for unit in range(3):
        loads.append(
            pltpu.make_async_copy(
                weights.at[:, pl.ds(STARTS[unit], WIDTHS[unit])],
                shard(unit, dp),
                local_sem.at[unit],
            )
        )
    loads.append(pltpu.make_async_copy(o_weight, shard(OUT, dp), local_sem.at[OUT]))
    load_rows = pltpu.make_async_copy(states, rows_in, local_sem.at[4])
    loads[0].start()
    load_rows.start()
    for load in loads[1:]:
        load.start()

    pl.semaphore_wait(barrier, len(partners))

    sends = []
    norm_copies = []
    stores = []

    def send(src, dst, send_sem, recv_sem, device, sends=sends):
        copy = pltpu.make_async_remote_copy(
            src_ref=src,
            dst_ref=dst,
            send_sem=send_sem,
            recv_sem=recv_sem,
            device_id=device,
            device_id_type=MESH,
        )
        copy.start()
        sends.append(copy)
        return copy

    def await_recv(dst, recv_sem):
        pltpu.make_async_remote_copy(
            src_ref=dst,
            dst_ref=dst,
            send_sem=pair_send.at[0],
            recv_sem=recv_sem,
            device_id=sibling,
            device_id_type=MESH,
        ).wait_recv()

    def flavour(half):
        return z_lo + half * (1 - 2 * z_lo)

    def ring_pos(half):
        turn = flavour(half)
        return (x + turn * (y - x), y + turn * (x - y))

    def ring_place(half, first, second):
        turn = flavour(half)
        first, second = wrap(first), wrap(second)
        return (first + turn * (second - first), second + turn * (first - second))

    def ring_device(half, first, second):
        px, py = ring_place(half, first, second)
        return (px * 8 + py * 2 + z_lo, tensor)

    def ring_shard(unit, half, first, second):
        px, py = ring_place(half, first, second)
        return shard(unit, px * 8 + py * 2 + flavour(half))

    def ring_recv_sem(unit, half, a, b):
        return ring_recv.at[(unit * 2 + half) * 16 + a * 4 + b]

    def ring_send_sem(unit, half, index):
        return ring_send.at[(unit * 2 + half) * 16 + index]

    def pair_start(unit):
        loads[unit].wait()
        send(shard(unit, dp), shard(unit, dp), pair_send.at[unit], pair_recv.at[unit], pair)

    def spread(unit, half, a):
        first, second = ring_pos(half)
        piece = ring_shard(unit, half, first + a, second)
        for index, (step, b) in enumerate(((1, 3), (-1, 1))):
            send(
                piece,
                piece,
                ring_send_sem(unit, half, 3 + 2 * a + index),
                ring_recv_sem(unit, half, a, b),
                ring_device(half, first, second + step),
            )

    def ring_open(unit, half):
        first, second = ring_pos(half)
        piece = ring_shard(unit, half, first, second)
        if half == 1:
            await_recv(piece, pair_recv.at[unit])
        for index, (step, a) in enumerate(((1, 3), (-1, 1))):
            send(
                piece,
                piece,
                ring_send_sem(unit, half, index),
                ring_recv_sem(unit, half, a, 0),
                ring_device(half, first + step, second),
            )
        spread(unit, half, 0)

    def ring_head(unit, half, a):
        first, second = ring_pos(half)
        piece = ring_shard(unit, half, first + a, second)
        await_recv(piece, ring_recv_sem(unit, half, a, 0))
        upward = unit != OUT and (half + (unit in (1, 2))) % 2 == 0
        if a == (3 if upward else 1):
            step = 1 if upward else -1
            send(
                piece,
                piece,
                ring_send_sem(unit, half, 2),
                ring_recv_sem(unit, half, 2, 0),
                ring_device(half, first + step, second),
            )

    def ring_first(unit, half, a):
        ring_head(unit, half, a)
        spread(unit, half, a)

    def ring_second(unit, half, a, upward=None):
        first, second = ring_pos(half)
        upward = a in (0, 3) if upward is None else upward
        for b in (1, 3):
            piece = ring_shard(unit, half, first + a, second + b)
            await_recv(piece, ring_recv_sem(unit, half, a, b))
            if b == (3 if upward else 1):
                step = 1 if upward else -1
                send(
                    piece,
                    piece,
                    ring_send_sem(unit, half, 11 + a),
                    ring_recv_sem(unit, half, a, 2),
                    ring_device(half, first, second + step),
                )

    def ring_last(unit, half, a):
        first, second = ring_pos(half)
        piece = ring_shard(unit, half, first + a, second + 2)
        await_recv(piece, ring_recv_sem(unit, half, a, 2))

    def half_of(turn):
        return turn + z_lo * (1 - 2 * turn)

    def turn_last(unit, turn, a):
        half = half_of(turn)
        px, py = (wrap(x + a), wrap(y + 2)) if turn == 0 else (wrap(x + 2), wrap(y + a))
        await_recv(shard(unit, px * 8 + py * 2 + turn), ring_recv_sem(unit, half, a, 2))

    def norm_rows(block, step):
        start = pl.multiple_of(block * BLOCK + step * NORM_ROWS, NORM_ROWS)
        return normed.at[pl.ds(start, NORM_ROWS), :]

    def norm_step(step):
        full = rows_in[step * NORM_ROWS : (step + 1) * NORM_ROWS, :].astype(jnp.float32)
        scale = lax.rsqrt(jnp.mean(full * full, axis=-1, keepdims=True) + norm_eps)
        piece = norm_rows(tensor, step)
        piece[...] = (full * scale * norm_gain[...]).astype(jnp.bfloat16)
        send(piece, piece, norm_send.at[4 + step], norm_recv.at[4 + step], sibling, norm_copies)

    def norm_beside(step):
        await_recv(norm_rows(z_hi * 2 + 1 - core, step), norm_recv.at[4 + step])

    def half_rows(chip, step, side):
        start = pl.multiple_of(chip * 512 + step * 128 + side * 64, 64)
        return normed.at[pl.ds(start, 64), :]

    def norm_across(step):
        piece = half_rows(near, step, core)
        send(piece, piece, norm_send.at[step], norm_recv.at[step], across, norm_copies)

    def norm_forward(step):
        piece = half_rows(far, step, core)
        await_recv(piece, norm_recv.at[step])
        send(piece, piece, norm_send.at[8 + step], norm_recv.at[8 + step], sibling, norm_copies)

    def norm_far(step):
        await_recv(half_rows(far, step, 1 - core), norm_recv.at[8 + step])

    def turned(raw, gain, start, rows):
        scale = lax.rsqrt(jnp.mean(raw * raw, axis=-1, keepdims=True) + norm_eps)
        flat = raw * scale * gain
        return (
            flat * cosine[pl.ds(start, rows), :]
            + pltpu.roll(flat, 64, 1) * sine[pl.ds(start, rows), :]
        ).astype(jnp.bfloat16)

    def project(unit, chip, offset, rows):
        start = pl.multiple_of(chip * 512 + offset, 128)
        raw = jnp.dot(
            normed[pl.ds(start, rows), :], units[unit][...], preferred_element_type=jnp.float32
        )
        for column in range(WIDTHS[unit] // 128):
            part = raw[:, column * 128 : (column + 1) * 128]
            head = STARTS[unit] // 128 + column - 2
            if head == -2:
                keys[pl.ds(start, rows), :] = turned(part, qk_gain[1:2, :], start, rows)
            elif head == -1:
                values[pl.ds(start, rows), :] = part.astype(jnp.bfloat16)
            else:
                queries[head, pl.ds(start, rows), :] = turned(part, qk_gain[0:1, :], start, rows)

    def begin_of(row):
        begin, bound = jnp.zeros_like(row), 0
        for index in range(8):
            bound = bound + lengths[0, index]
            begin = jnp.where(row >= bound, bound, begin)
        return begin

    def make_tables(block):
        row = block * BLOCK + lax.broadcasted_iota(jnp.int32, (BLOCK, 128), 0)
        angle = (row - begin_of(row)).astype(jnp.float32) * freq[...]
        lane = lax.broadcasted_iota(jnp.int32, (BLOCK, 128), 1)
        rows = slice(block * BLOCK, (block + 1) * BLOCK)
        cosine[rows, :] = jnp.cos(angle)
        sine[rows, :] = jnp.where(lane < 64, -1.0, 1.0) * jnp.sin(angle)

    def make_bias(block):
        low = max(block - 2, 0) * BLOCK
        row = block * BLOCK + lax.broadcasted_iota(jnp.int32, (BLOCK, 1), 0)
        column = low + lax.broadcasted_iota(jnp.int32, (BLOCK, WINDOW), 1)
        bias[block] = jnp.where((column >= begin_of(row)) & (column <= row), 0.0, -1e30)

    def attend(block, first_head, heads):
        start = pl.multiple_of(block * BLOCK, BLOCK)
        low = pl.multiple_of(jnp.maximum(block - 2, 0) * BLOCK, BLOCK)

        def two_heads(index, carry):
            head = first_head + 2 * index
            pair_of = queries[pl.ds(head, 2), pl.ds(start, BLOCK), :].reshape(2 * BLOCK, 128)
            scores = lax.dot_general(
                pair_of,
                keys[pl.ds(low, WINDOW), :],
                (((1,), (1,)), ((), ())),
                preferred_element_type=jnp.float32,
            ).reshape(2, BLOCK, WINDOW)
            scores = scores * (128 ** (-0.5) * LOG2_E) + bias[block][None]
            raised = jnp.exp2(scores - jnp.max(scores, axis=-1, keepdims=True))
            total = jnp.sum(raised, axis=-1, keepdims=True)
            mixed = jnp.dot(
                raised.astype(jnp.bfloat16).reshape(2 * BLOCK, WINDOW),
                values[pl.ds(low, WINDOW), :],
                preferred_element_type=jnp.float32,
            ).reshape(2, BLOCK, 128)
            mixed = (mixed / total).astype(jnp.bfloat16)
            for side in range(2):
                lanes = pl.ds(pl.multiple_of((head + side) * 128, 128), 128)
                context[pl.ds(start, BLOCK), lanes] = mixed[side]
            return carry

        lax.fori_loop(0, heads // 2, two_heads, 0, unroll=True)

    own_mine, own_other = normed.at[0:BLOCK, :], normed.at[BLOCK : 2 * BLOCK, :]

    def chunk_columns(index):
        order = ((0, 0), (0, 1), (1, 0), (1, 1), (3, 0), (3, 1), (2, 0), (2, 1))
        step, half = order[index]
        place = wrap(x + step) * 2 + lax.rem(y // 2 + half, 2)
        return pl.multiple_of(place * CHUNK, 128)

    def column_of(ref, index):
        return ref.at[:, pl.ds(chunk_columns(index), CHUNK)]

    def out_part(block, target, index):
        start = pl.multiple_of(block * BLOCK, BLOCK)
        part = lax.dot_general(
            context[pl.ds(start, BLOCK), :],
            wo[pl.ds(chunk_columns(index), CHUNK), :],
            (((1,), (1,)), ((), ())),
            preferred_element_type=jnp.float32,
        )
        column_of(target, index)[...] = part.astype(jnp.bfloat16)

    def far_half(block, side):
        return far_parts.at[pl.ds(pl.multiple_of(block * BLOCK + side * 128, 128), 128), :]

    def sib_half(block):
        return sib_far.at[block * 128 : (block + 1) * 128, :]

    def out_far(index, block):
        out_part(far * 2 + block, far_parts.at[block * BLOCK : (block + 1) * BLOCK, :], index)
        send(
            column_of(far_half(block, 1 - core), index),
            column_of(sib_half(block), index),
            out_send.at[index * 2 + block],
            out_recv.at[index * 2 + block],
            sibling,
        )

    def sum_half(side):
        return far_sum.at[pl.ds(pl.multiple_of(side * 128, 128), 128), :]

    def out_far_sum(index, block):
        await_recv(column_of(sib_half(block), index), out_recv.at[index * 2 + block])
        piece = column_of(far_half(block, core), index)
        piece[...] = (
            piece[...].astype(jnp.float32)
            + column_of(sib_half(block), index)[...].astype(jnp.float32)
        ).astype(jnp.bfloat16)
        send(
            piece,
            column_of(sum_half(core), index),
            out_send.at[16 + index * 2 + block],
            out_recv.at[16 + index * 2 + core],
            (dp, far * 2 + block),
        )

    def out_own(index):
        out_part(near * 2 + 1 - core, own_other, index)
        out_part(near * 2 + core, own_mine, index)
        send(
            column_of(own_other, index),
            column_of(sib_own, index),
            out_send.at[32 + index],
            out_recv.at[32 + index],
            sibling,
        )

    def out_final(index):
        await_recv(column_of(sib_own, index), out_recv.at[32 + index])
        for side in range(2):
            await_recv(column_of(sum_half(side), index), out_recv.at[16 + index * 2 + side])
        total = column_of(own_mine, index)[...].astype(jnp.float32)
        total = total + column_of(sib_own, index)[...].astype(jnp.float32)
        total = total + column_of(far_sum, index)[...].astype(jnp.float32)
        total = total + column_of(rows_in, index)[...].astype(jnp.float32)
        column_of(rows_in, index)[...] = total.astype(jnp.bfloat16)
        copy = pltpu.make_async_copy(
            column_of(rows_in, index), column_of(scored, index), store_sem.at[index]
        )
        copy.start()
        stores.append(copy)

    def both(step, unit, *rest):
        for half in range(2):
            step(unit, half, *rest)

    along_x, along_y = half_of(0), half_of(1)
    mate, other = 1 + 2 * lax.rem(y, 2), 3 - 2 * lax.rem(y, 2)

    pair_start(0)
    ring_open(0, 0)
    load_rows.wait()
    for step in range(NORM_STEPS):
        norm_step(step)
    ring_open(0, 1)
    pair_start(1)
    pair_start(2)
    for step in range(NORM_STEPS):
        norm_beside(step)
    norm_across(0)
    both(ring_first, 0, 1)
    both(ring_first, 0, 3)
    norm_across(1)
    both(ring_first, 0, 2)
    both(ring_open, 1)
    both(ring_second, 0, 0)
    both(ring_first, 1, 1)
    pair_start(OUT)
    norm_across(2)
    make_tables(0)
    make_bias(0)
    both(ring_second, 0, 1)
    both(ring_first, 1, 3)
    make_tables(1)
    make_bias(1)
    both(ring_second, 0, 3)
    both(ring_first, 1, 2)
    norm_across(3)
    make_tables(2)
    make_bias(2)
    both(ring_second, 0, 2)
    both(ring_open, 2)
    make_tables(3)
    make_bias(3)
    norm_forward(0)
    for a in range(4):
        both(ring_last, 0, a)
    both(ring_second, 1, 0)
    both(ring_first, 2, 1)
    project(0, near, 0, 256)
    both(ring_second, 1, 1)
    both(ring_first, 2, 3)
    project(0, near, 256, 256)
    both(ring_second, 1, 3)
    both(ring_first, 2, 2)
    norm_forward(1)
    both(ring_second, 1, 2)
    norm_far(0)
    norm_far(1)
    project(0, far, 0, 256)
    for a in range(4):
        both(ring_last, 1, a)
    both(ring_second, 2, 0)
    project(1, near, 0, 256)
    both(ring_second, 2, 1)
    both(ring_second, 2, 3)
    both(ring_second, 2, 2)
    ring_open(OUT, 0)
    project(1, near, 256, 256)
    project(1, far, 0, 256)
    ring_open(OUT, 1)
    norm_forward(2)
    attend(far * 2, 0, 4)
    for a in range(4):
        both(ring_last, 2, a)
    project(2, far, 0, 256)
    attend(far * 2, 4, 2)
    ring_head(OUT, 0, 1)
    ring_head(OUT, 0, 3)
    ring_second(OUT, 0, 0)
    norm_forward(3)
    attend(far * 2, 6, 2)
    norm_far(2)
    norm_far(3)
    project(0, far, 256, 256)
    ring_head(OUT, 1, 1)
    ring_head(OUT, 1, 3)
    ring_second(OUT, 1, 0)
    out_far(0, 0)
    spread(OUT, along_x, 1)
    spread(OUT, along_y, mate)
    project(1, far, 256, 256)
    out_far_sum(0, 0)
    attend(far * 2 + 1, 0, 4)
    project(2, far, 256, 256)
    ring_head(OUT, 0, 2)
    spread(OUT, along_x, 3)
    spread(OUT, along_y, other)
    ring_head(OUT, 1, 2)
    turn_last(OUT, 0, 0)
    out_far(1, 0)
    spread(OUT, along_y, 2)
    attend(far * 2 + 1, 4, 4)
    out_far_sum(1, 0)
    out_far(0, 1)
    out_far(1, 1)
    out_far_sum(0, 1)
    project(2, near, 0, 256)
    out_far_sum(1, 1)
    project(2, near, 256, 256)
    ring_second(OUT, along_x, 1)
    ring_second(OUT, along_y, mate, False)
    out_far(2, 0)
    out_far(2, 1)
    out_far_sum(2, 0)
    out_far_sum(2, 1)
    ring_second(OUT, along_x, 3)
    spread(OUT, along_x, 2)
    out_far(4, 0)
    out_far(4, 1)
    ring_second(OUT, along_y, other, True)
    out_far_sum(4, 0)
    out_far_sum(4, 1)
    attend(near * 2, 0, 8)
    turn_last(OUT, 0, 1)
    ring_second(OUT, along_y, 2)
    for block in range(2):
        out_far(3, block)
    turn_last(OUT, 0, 3)
    for block in range(2):
        out_far(5, block)
        out_far_sum(3, block)
    for block in range(2):
        out_far_sum(5, block)
    attend(near * 2 + 1, 0, 8)
    ring_second(OUT, along_x, 2, True)
    for copy in norm_copies:
        copy.wait_send()
    for index in range(2):
        out_own(index)
    turn_last(OUT, 0, 2)
    for a in range(4):
        turn_last(OUT, 1, a)
    for block in range(2):
        out_far(6, block)
    for block in range(2):
        out_far(7, block)
        out_far_sum(6, block)
    for block in range(2):
        out_far_sum(7, block)
    for index in range(2, STEPS):
        out_own(index)
    for index in range(STEPS):
        out_final(index)
    for copy in sends:
        copy.wait_send()
    for copy in stores:
        copy.wait()


def layer(weights, o_weight, states, norm_gain, qk_gain, lengths, freq):
    bf16, f32 = jnp.bfloat16, jnp.float32
    width = states.shape[1]
    tokens = 4 * BLOCK
    vmem = pl.BlockSpec(memory_space=pltpu.VMEM)
    hbm = pl.BlockSpec(memory_space=pl.ANY)
    return pl.pallas_call(
        layer_kernel,
        out_shape=jax.ShapeDtypeStruct(states.shape, bf16),
        in_specs=[hbm, hbm, hbm, vmem, vmem, pl.BlockSpec(memory_space=pltpu.SMEM), vmem],
        out_specs=hbm,
        scratch_shapes=[
            *[pltpu.VMEM((width, columns), bf16) for columns in WIDTHS],
            pltpu.VMEM((tokens, width), bf16),
            pltpu.VMEM((BLOCK, width), bf16),
            pltpu.VMEM((8, tokens, 128), bf16),
            pltpu.VMEM((tokens, 128), bf16),
            pltpu.VMEM((tokens, 128), bf16),
            pltpu.VMEM((tokens, 1024), bf16),
            pltpu.VMEM((4, BLOCK, WINDOW), f32),
            pltpu.VMEM((tokens, 128), f32),
            pltpu.VMEM((tokens, 128), f32),
            pltpu.VMEM((2 * BLOCK, width), bf16),
            *[pltpu.VMEM((BLOCK, width), bf16) for _ in range(3)],
            pltpu.SemaphoreType.DMA((5,)),
            pltpu.SemaphoreType.DMA((128,)),
            pltpu.SemaphoreType.DMA((128,)),
            pltpu.SemaphoreType.DMA((4,)),
            pltpu.SemaphoreType.DMA((4,)),
            pltpu.SemaphoreType.DMA((12,)),
            pltpu.SemaphoreType.DMA((12,)),
            pltpu.SemaphoreType.DMA((40,)),
            pltpu.SemaphoreType.DMA((40,)),
            pltpu.SemaphoreType.DMA((STEPS,)),
        ],
        compiler_params=pltpu.CompilerParams(
            collective_id=1, has_side_effects=True, vmem_limit_bytes=62 * 2**20
        ),
        cost_estimate=pl.CostEstimate(
            flops=30_000_000_000, bytes_accessed=10_000_000, transcendentals=5_000_000
        ),
        name="layer",
    )(weights, o_weight, states, norm_gain, qk_gain, lengths, freq)


def copy_kernel(source, target):
    target[...] = source[...]


def copied(rows):
    spec = pl.BlockSpec((rows.shape[0] // 2, rows.shape[1]), lambda step: (step, 0))
    return pl.pallas_call(
        copy_kernel,
        grid=(2,),
        out_shape=jax.ShapeDtypeStruct(rows.shape, rows.dtype),
        in_specs=[spec],
        out_specs=spec,
        compiler_params=pltpu.CompilerParams(vmem_limit_bytes=62 * 2**20),
        name="copied",
    )(rows)


def per_device(
    states,
    lengths,
    norm_gain,
    qk_gain,
    q_master,
    q_grad,
    q_moments,
    kv_master,
    kv_grad,
    kv_moments,
    o_master,
    o_grad,
    o_moments,
):
    q_new, q_moments_new, kv_new, kv_moments_new, o_new, o_moments_new, weights, o_weight = adam(
        q_master,
        q_grad,
        q_moments,
        kv_master,
        kv_grad,
        kv_moments,
        o_master,
        o_grad,
        o_moments,
    )
    head = qk_gain.shape[1]
    half = np.arange(head // 2) * 2.0 / head
    freq = np.tile(rope_base**-half, 2)[None, :].astype(np.float32)
    scored = layer(
        weights, o_weight, states, norm_gain[None, :], qk_gain, lengths, jnp.asarray(freq)
    )
    return (copied(scored), q_new, q_moments_new, kv_new, kv_moments_new, o_new, o_moments_new)


def solution(mesh):
    return jax.shard_map(
        per_device,
        mesh=mesh,
        in_specs=(
            P(("dp", "tensor"), None),
            P("dp", None),
            P(),
            P(),
            P("dp", "tensor"),
            P("dp", "tensor"),
            P(None, "dp", "tensor"),
            P(None, "dp", "tensor"),
            P(None, "dp", "tensor"),
            P(None, None, "dp", "tensor"),
            P("dp", "tensor"),
            P("dp", "tensor"),
            P(None, "dp", "tensor"),
        ),
        out_specs=(
            P(("dp", "tensor"), None),
            P("dp", "tensor"),
            P(None, "dp", "tensor"),
            P(None, "dp", "tensor"),
            P(None, None, "dp", "tensor"),
            P("dp", "tensor"),
            P(None, "dp", "tensor"),
        ),
        check_vma=False,
    )
```
